32 devices in a mesh: groups: 2 (over x), chan: 8 (over z, y), tm: 2 (over core).
Axes of the slice: x: 2, y: 2, z: 4, core: 2. Of those that a mesh axis runs over, the one named last changes fastest.
Arguments:
- traces: bfloat16 [2048, 2, 1024], P(('groups', 'chan'), 'tm'), parts along dimension 0, may hold values from -6 to 6
- fir_taps: bfloat16 [64], replicated, may hold values from -0.75 to 0.75
- pair_blocks: int32 [64, 2], P(('groups', 'chan')), parts along dimension 0, may hold values from 0 to 7, as said below
- pair_count: int32 [16], P(('groups', 'chan')), parts along dimension 0, may hold values from 1 to 4, as said below
Outputs:
- stacks: float32 [64, 128, 65, 128], P(('groups', 'chan'), 'tm'), parts along dimension 0
The draws below stay inside these ranges and needn't reach their ends.
There are 2 independent parts, one for each index of `groups`. The reference program is written for one: setup_inputs(seed, part) draws one part's arguments, and reference() takes and returns one part's arrays. A program takes and returns all parts, laid end to end along the dimension named above; an argument that names none is the same for every part. Nothing has to cross between parts.
Inputs may be any that keep to these rules, and one draw needn't show every extreme that they name: `pair_blocks`: both blocks of a slot of owner o lie within 2 blocks of o; the first slot of every owner has source max(o - 2, 0) and partner min(o + 2, 7). `pair_count`: some owner uses all its slots.
All inputs are finite; a program needn't handle non-finite values.
Results may differ from the reference program's by a relative error of at most 0.0027.
Values may be sent and summed in bfloat16 or wider, within the bound.
No kernel may reach another device: no remote copies, remote signals or barrier semaphores. Data moves between devices by JAX's collectives and lax.ppermute only.
A program may use at most 128 MiB of HBM per device.

```python
import jax
import jax.numpy as jnp
from jax import lax

CH = 128
WIN = 1024
TAPS = 64
LAG = 32
REACH = 2
PAIR_CAP = 4
NB = 8
CHANNELS = 1024
NWIN = 2
PAIRS = 32


def draw_pair_count(key, part):
    key = jax.random.fold_in(key, 11)
    counts = jax.random.randint(key, (NB,), 1, PAIR_CAP + 1)
    busiest = jax.random.randint(jax.random.fold_in(key, 1), (), 0, NB)
    return counts.at[busiest].set(PAIR_CAP).astype(jnp.int32)


def draw_pair_blocks(key, part):
    key = jax.random.fold_in(key, 23)
    slots = jnp.arange(PAIRS, dtype=jnp.int32)
    owner = slots // PAIR_CAP
    offsets = jax.random.randint(key, (PAIRS, 2), -REACH, REACH + 1)
    first = slots % PAIR_CAP == 0
    edge = jnp.array([-REACH, REACH], dtype=jnp.int32)[None, :]
    offsets = jnp.where(first[:, None], edge, offsets)
    return jnp.clip(owner[:, None] + offsets, 0, NB - 1).astype(jnp.int32)


def block_scale(stream_key, extent, split, low, top_value):
    factor_of = 1.0
    for position, blocks in split:
        draws = jax.random.uniform(jax.random.fold_in(jax.random.fold_in(stream_key, 6), position), (blocks,), jnp.float32, low / len(split), top_value / len(split))
        factor_of = factor_of * jnp.repeat(jnp.exp(draws), extent[position] // blocks).reshape((-1,) + (1,) * (len(extent) - 1 - position))
    return factor_of


def bell_draw(rng, shape, deviation, most, pieces=(), kind=jnp.bfloat16):
    entries = jax.random.normal(rng, shape, jnp.float32) * deviation
    if len(pieces) > 0:
        entries = block_scale(rng, shape, pieces, -0.22, 0.18) * entries
    return jnp.clip(entries, min=-most, max=most).astype(kind)


def setup_inputs(seed: int = 0, part: int = 0) -> dict:
    arg_keys = jax.random.split(jax.random.key(seed), 5)
    part_splits = jax.random.split(jax.random.fold_in(arg_keys[4], part), 5)
    return {
        "traces": bell_draw(part_splits[0], (CHANNELS, NWIN, WIN), 1.0, 6.0, ((0, 8), (1, 2))),
        "fir_taps": bell_draw(arg_keys[1], (TAPS,), TAPS ** -0.5, 0.75),
        "pair_blocks": draw_pair_blocks(jax.random.fold_in(jax.random.fold_in(arg_keys[4], part), 71), part),
        "pair_count": draw_pair_count(jax.random.fold_in(jax.random.fold_in(arg_keys[4], part), 71), part),
    }


def fir_matrix(fir_taps, length):
    first = jnp.arange(length, dtype=jnp.int32)[:, None]
    second = jnp.arange(length, dtype=jnp.int32)[None, :]
    offset = second - first
    picked = fir_taps[jnp.clip(offset, 0, fir_taps.shape[0] - 1)]
    inside = (offset >= 0) & (offset < fir_taps.shape[0])
    return jnp.where(inside, picked, jnp.zeros_like(picked)).astype(jnp.bfloat16)

def correlate(source_rows, partner_rows, lag):
    length = partner_rows.shape[-1]
    padded = jnp.pad(partner_rows, ((0, 0), (0, 0), (lag, lag))).astype(jnp.float32)
    source_wide = source_rows.astype(jnp.float32)

    def one_lag(step):
        moved = lax.dynamic_slice_in_dim(padded, step, length, 2)
        return jnp.einsum('iwt,jwt->ij', source_wide, moved)
    result = lax.map(one_lag, jnp.arange(2 * lag + 1, dtype=jnp.int32))
    return jnp.transpose(result, (1, 0, 2))

def reference(traces, fir_taps, pair_blocks, pair_count):
    matrix = fir_matrix(fir_taps, WIN)
    filtered = jnp.dot(traces.reshape(CHANNELS * NWIN, WIN), matrix, preferred_element_type=jnp.float32)
    meansq = lax.optimization_barrier(jnp.mean(filtered * filtered, axis=-1, keepdims=True))
    unit = (filtered * lax.rsqrt(meansq + 1e-06)).astype(jnp.bfloat16).reshape(NB, CH, NWIN, WIN)
    scale = float(NWIN * WIN) ** (-0.5)

    def one_slot(index):
        source_rows = unit[pair_blocks[index, 0]]
        partner_rows = unit[pair_blocks[index, 1]]
        raw = correlate(source_rows, partner_rows, LAG) * scale
        valid = index % PAIR_CAP < pair_count[index // PAIR_CAP]
        return jnp.where(valid, raw, jnp.zeros_like(raw))
    return lax.map(one_slot, jnp.arange(PAIRS, dtype=jnp.int32))
```

```python
import functools

import jax
import jax.numpy as jnp
from jax import lax
from jax.experimental import pallas as pl
from jax.experimental.pallas import tpu as pltpu
from jax.sharding import PartitionSpec as P

LAG = 32
REACH = 2
NEAR = 2 * REACH + 1
FINE = 8
COARSE = LAG // FINE
LANES = 128
TILE = 256


def passed_along(block, axis, distance):
    devices = range(lax.axis_size(axis))
    route = [(i - distance, i) for i in devices if i - distance in devices]
    return lax.ppermute(block, axis, route)


def swapped(block, axis):
    return lax.ppermute(block, axis, [(0, 1), (1, 0)])


def shifted(rows, amount):
    if amount == 0:
        return rows
    length = rows.shape[-1]
    moved = pltpu.roll(rows, amount % length, 1)
    edge = slice(0, LANES) if amount > 0 else slice(length - LANES, length)
    lane = lax.broadcasted_iota(jnp.int32, (rows.shape[0], LANES), 1)
    keep = lane >= amount if amount > 0 else lane < LANES + amount
    cut = jnp.where(keep, moved[:, edge], jnp.zeros((), rows.dtype))
    if amount > 0:
        return jnp.concatenate([cut, moved[:, LANES:]], axis=1)
    return jnp.concatenate([moved[:, : length - LANES], cut], axis=1)


def contract_lanes(left, right):
    return lax.dot_general(
        left, right, (((1,), (1,)), ((), ())), preferred_element_type=jnp.float32
    )


def kernel(scale, pairs_ref, count_ref, taps_ref, mine_ref, other_ref, out_ref,
           here_ref, after_ref, unit_ref, left_ref, right_ref):
    slot = pl.program_id(0)
    length = mine_ref.shape[-1]
    half_rows = out_ref.shape[2]

    @pl.when(slot == 0)
    def _():
        taps = taps_ref[...]
        wide = jnp.concatenate(
            [taps, jnp.zeros((1, TILE - taps.shape[1]), jnp.float32)], axis=1
        )
        band = pltpu.roll(
            jnp.broadcast_to(wide, (TILE, TILE)), 0, 1, stride=1, stride_axis=0
        )
        row = lax.broadcasted_iota(jnp.int32, (TILE, TILE), 0)
        column = lax.broadcasted_iota(jnp.int32, (TILE, TILE), 1)
        here_ref[...] = jnp.where(column >= row, band, 0.0).astype(jnp.bfloat16)
        after_ref[...] = jnp.where(column < row, band, 0.0).astype(jnp.bfloat16)

        for window, source in enumerate((mine_ref, other_ref)):
            for block in range(NEAR):
                pieces = []
                for start in range(0, length, TILE):
                    piece = jnp.dot(
                        source[block, :, start : start + TILE], here_ref[...],
                        preferred_element_type=jnp.float32,
                    )
                    if start > 0:
                        piece += jnp.dot(
                            source[block, :, start - TILE : start], after_ref[...],
                            preferred_element_type=jnp.float32,
                        )
                    pieces.append(piece)
                filtered = jnp.concatenate(pieces, axis=1)
                meansq = jnp.mean(filtered * filtered, axis=-1, keepdims=True)
                unit_ref[block, :, window * length : (window + 1) * length] = (
                    filtered * lax.rsqrt(meansq + 1e-06)
                ).astype(jnp.bfloat16)

    owner = lax.axis_index("chan")
    first_row = pl.multiple_of(lax.axis_index("tm") * half_rows, half_rows)
    source = pairs_ref[slot, 0] - owner + REACH
    partner = pairs_ref[slot, 1] - owner + REACH
    factor = jnp.where(slot < count_ref[0], scale, 0.0)
    channels = mine_ref.shape[1]

    for sign in (1, -1):
        for window in range(2):
            span = slice(window * length, (window + 1) * length)
            rows = unit_ref[source, pl.ds(first_row, half_rows), span]
            steps = range(FINE + 1) if sign > 0 else range(-FINE, 0)
            for place, step in enumerate(steps):
                left_ref[place * half_rows : (place + 1) * half_rows, span] = shifted(rows, step)
            rows = unit_ref[partner, :, span]
            for place in range(COARSE):
                right_ref[place * channels : (place + 1) * channels, span] = shifted(
                    rows, -sign * FINE * place
                )
        for pair in range(0, COARSE, 2):
            tall = FINE + 1 if sign > 0 and pair + 2 == COARSE else FINE
            result = contract_lanes(
                left_ref[: tall * half_rows, :],
                right_ref[pair * channels : (pair + 2) * channels, :],
            )
            for within in range(2):
                for place in range(tall):
                    if place == FINE and within == 0:
                        continue
                    coarse = sign * FINE * (pair + within)
                    lag = LAG + coarse + (place if sign > 0 else place - FINE)
                    out_ref[0, lag] = factor * result[
                        place * half_rows : (place + 1) * half_rows,
                        within * channels : (within + 1) * channels,
                    ]


def body(traces, fir_taps, pair_blocks, pair_count):
    rows, windows, length = traces.shape
    block = traces.reshape(rows, length)
    halves = lax.axis_size("tm")
    near = [
        block if offset == 0 else passed_along(block, "chan", -offset)
        for offset in range(-REACH, REACH + 1)
    ]
    mine = jnp.stack(near, axis=0)
    other = swapped(mine, "tm")
    cap = pair_blocks.shape[0]
    lags = 2 * LAG + 1
    half_rows = rows // halves
    scale = float(windows * halves * length) ** (-0.5)
    smem = pl.BlockSpec(memory_space=pltpu.SMEM)
    whole = lambda shape: pl.BlockSpec(shape, lambda slot: (0,) * len(shape))
    result = pl.pallas_call(
        functools.partial(kernel, scale),
        grid=(cap,),
        out_shape=jax.ShapeDtypeStruct((cap, lags, half_rows, rows), jnp.float32),
        in_specs=[
            smem,
            smem,
            whole((1, fir_taps.shape[0])),
            whole(mine.shape),
            whole(mine.shape),
        ],
        out_specs=pl.BlockSpec((1, lags, half_rows, rows), lambda slot: (slot, 0, 0, 0)),
        scratch_shapes=[
            pltpu.VMEM((TILE, TILE), jnp.bfloat16),
            pltpu.VMEM((TILE, TILE), jnp.bfloat16),
            pltpu.VMEM((NEAR, rows, halves * length), jnp.bfloat16),
            pltpu.VMEM(((FINE + 1) * half_rows, halves * length), jnp.bfloat16),
            pltpu.VMEM((COARSE * rows, halves * length), jnp.bfloat16),
        ],
        compiler_params=pltpu.CompilerParams(vmem_limit_bytes=48 * 1024 * 1024),
        cost_estimate=pl.CostEstimate(
            flops=2 * cap * lags * half_rows * rows * halves * length,
            bytes_accessed=cap * lags * half_rows * rows * 4 + 4 * mine.size,
            transcendentals=0,
        ),
    )(pair_blocks, pair_count, fir_taps.astype(jnp.float32)[None, :], mine, other)
    return jnp.transpose(result, (0, 2, 1, 3))


def solution(mesh):
    return jax.shard_map(
        body,
        mesh=mesh,
        in_specs=(
            P(("groups", "chan"), "tm", None),
            P(),
            P(("groups", "chan"), None),
            P(("groups", "chan")),
        ),
        out_specs=P(("groups", "chan"), "tm", None, None),
        check_vma=False,
    )
```

```python
import functools

import jax
import jax.numpy as jnp
from jax import lax
from jax.experimental import pallas as pl
from jax.experimental.pallas import tpu as pltpu
from jax.sharding import PartitionSpec as P

LAG = 32
REACH = 2
NEAR = 2 * REACH + 1
FINE = 8
COARSE = LAG // FINE
LANES = 128
TILE = 256


def passed(block, axis, target):
    size = lax.axis_size(axis)
    route = [(i, target(i)) for i in range(size) if 0 <= target(i) < size]
    return lax.ppermute(block, axis, route)


def partner_of(i):
    return i + 1 if i % 2 == 0 else i - 1


def diagonal_of(i):
    return i - 1 if i % 2 == 0 else i + 1


def place_of(block, owner):
    offset = block - owner
    side = jnp.where(offset == 1 - 2 * lax.rem(owner, 2), 3, 4)
    return jnp.where(
        offset == 0, 0, jnp.where(offset == -REACH, 1, jnp.where(offset == REACH, 2, side))
    )


def shifted(rows, amount):
    if amount == 0:
        return rows
    length = rows.shape[-1]
    moved = pltpu.roll(rows, amount % length, 1)
    edge = slice(0, LANES) if amount > 0 else slice(length - LANES, length)
    lane = lax.broadcasted_iota(jnp.int32, (rows.shape[0], LANES), 1)
    keep = lane >= amount if amount > 0 else lane < LANES + amount
    cut = jnp.where(keep, moved[:, edge], jnp.zeros((), rows.dtype))
    if amount > 0:
        return jnp.concatenate([cut, moved[:, LANES:]], axis=1)
    return jnp.concatenate([moved[:, : length - LANES], cut], axis=1)


def contract_lanes(left, right):
    return lax.dot_general(
        left, right, (((1,), (1,)), ((), ())), preferred_element_type=jnp.float32
    )


def kernel(scale, pairs_ref, count_ref, taps_ref, *refs):
    near_refs, (out_ref, here_ref, after_ref, unit_ref, left_ref, right_ref) = (
        refs[: 2 * NEAR], refs[2 * NEAR :]
    )
    slot = pl.program_id(0)
    channels, length = near_refs[0].shape
    half_rows = out_ref.shape[2]

    @pl.when(slot == 0)
    def _():
        taps = taps_ref[...]
        wide = jnp.concatenate(
            [taps, jnp.zeros((1, TILE - taps.shape[1]), jnp.float32)], axis=1
        )
        band = pltpu.roll(
            jnp.broadcast_to(wide, (TILE, TILE)), 0, 1, stride=1, stride_axis=0
        )
        row = lax.broadcasted_iota(jnp.int32, (TILE, TILE), 0)
        column = lax.broadcasted_iota(jnp.int32, (TILE, TILE), 1)
        here_ref[...] = jnp.where(column >= row, band, 0.0).astype(jnp.bfloat16)
        after_ref[...] = jnp.where(column < row, band, 0.0).astype(jnp.bfloat16)

        for window in range(2):
            for block in range(NEAR):
                source = near_refs[window * NEAR + block]
                pieces = []
                for start in range(0, length, TILE):
                    piece = jnp.dot(
                        source[:, start : start + TILE], here_ref[...],
                        preferred_element_type=jnp.float32,
                    )
                    if start > 0:
                        piece += jnp.dot(
                            source[:, start - TILE : start], after_ref[...],
                            preferred_element_type=jnp.float32,
                        )
                    pieces.append(piece)
                filtered = jnp.concatenate(pieces, axis=1)
                meansq = jnp.mean(filtered * filtered, axis=-1, keepdims=True)
                unit_ref[block, :, window * length : (window + 1) * length] = (
                    filtered * lax.rsqrt(meansq + 1e-06)
                ).astype(jnp.bfloat16)

    owner = lax.axis_index("chan")
    first_row = pl.multiple_of(lax.axis_index("tm") * half_rows, half_rows)
    source = place_of(pairs_ref[slot, 0], owner)
    partner = place_of(pairs_ref[slot, 1], owner)
    factor = jnp.where(slot < count_ref[0], scale, 0.0)

    for sign in (1, -1):
        for window in range(2):
            span = slice(window * length, (window + 1) * length)
            rows = unit_ref[source, pl.ds(first_row, half_rows), span]
            steps = range(FINE + 1) if sign > 0 else range(-FINE, 0)
            for place, step in enumerate(steps):
                left_ref[place * half_rows : (place + 1) * half_rows, span] = shifted(rows, step)
            rows = unit_ref[partner, :, span]
            for place in range(COARSE):
                right_ref[place * channels : (place + 1) * channels, span] = shifted(
                    rows, -sign * FINE * place
                )
        for pair in range(0, COARSE, 2):
            tall = FINE + 1 if sign > 0 and pair + 2 == COARSE else FINE
            result = contract_lanes(
                left_ref[: tall * half_rows, :],
                right_ref[pair * channels : (pair + 2) * channels, :],
            )
            for within in range(2):
                for place in range(tall):
                    if place == FINE and within == 0:
                        continue
                    coarse = sign * FINE * (pair + within)
                    lag = LAG + coarse + (place if sign > 0 else place - FINE)
                    out_ref[0, lag] = factor * result[
                        place * half_rows : (place + 1) * half_rows,
                        within * channels : (within + 1) * channels,
                    ]


def body(traces, fir_taps, pair_blocks, pair_count):
    rows, windows, length = traces.shape
    block = traces.reshape(rows, length)
    halves = lax.axis_size("tm")
    swap = lambda array: passed(array, "tm", lambda i: 1 - i)
    other_own = swap(block)
    diagonal = passed(block, "chan", diagonal_of)
    below = passed(block, "chan", lambda i: i + REACH)
    above = passed(block, "chan", lambda i: i - REACH)
    partner = passed(block, "chan", partner_of)
    mine = [block, below, above, partner, diagonal]
    other = [other_own] + [swap(array) for array in mine[1:]]
    cap = pair_blocks.shape[0]
    lags = 2 * LAG + 1
    half_rows = rows // halves
    scale = float(windows * halves * length) ** (-0.5)
    smem = pl.BlockSpec(memory_space=pltpu.SMEM)
    vmem = pl.BlockSpec(memory_space=pltpu.VMEM)
    result = pl.pallas_call(
        functools.partial(kernel, scale),
        grid=(cap,),
        out_shape=jax.ShapeDtypeStruct((cap, lags, half_rows, rows), jnp.float32),
        in_specs=[
            smem,
            smem,
            vmem,
            *[vmem] * (2 * NEAR),
        ],
        out_specs=pl.BlockSpec((1, lags, half_rows, rows), lambda slot: (slot, 0, 0, 0)),
        scratch_shapes=[
            pltpu.VMEM((TILE, TILE), jnp.bfloat16),
            pltpu.VMEM((TILE, TILE), jnp.bfloat16),
            pltpu.VMEM((NEAR, rows, halves * length), jnp.bfloat16),
            pltpu.VMEM(((FINE + 1) * half_rows, halves * length), jnp.bfloat16),
            pltpu.VMEM((COARSE * rows, halves * length), jnp.bfloat16),
        ],
        compiler_params=pltpu.CompilerParams(vmem_limit_bytes=48 * 1024 * 1024),
        cost_estimate=pl.CostEstimate(
            flops=2 * cap * lags * half_rows * rows * halves * length,
            bytes_accessed=cap * lags * half_rows * rows * 4 + 4 * NEAR * block.size,
            transcendentals=0,
        ),
    )(pair_blocks, pair_count, fir_taps.astype(jnp.float32)[None, :], *mine, *other)
    return jnp.transpose(result, (0, 2, 1, 3))


def solution(mesh):
    return jax.shard_map(
        body,
        mesh=mesh,
        in_specs=(
            P(("groups", "chan"), "tm", None),
            P(),
            P(("groups", "chan"), None),
            P(("groups", "chan")),
        ),
        out_specs=P(("groups", "chan"), "tm", None, None),
        check_vma=False,
    )
```

```python
import functools

import jax
import jax.numpy as jnp
from jax import lax
from jax.experimental import pallas as pl
from jax.experimental.pallas import tpu as pltpu
from jax.sharding import PartitionSpec as P

LAG = 32
REACH = 2
NEAR = 2 * REACH + 1
FINE = 8
COARSE = LAG // FINE
LANES = 128
TILE = 256
CHUNKS = 4
OWN, PARTNER, BELOW, ABOVE, DIAGONAL = range(NEAR)


def passed(block, axis, target):
    size = lax.axis_size(axis)
    route = [(i, target(i)) for i in range(size) if 0 <= target(i) < size]
    return lax.ppermute(block, axis, route)


def partner_of(i):
    return i + 1 if i % 2 == 0 else i - 1


def diagonal_of(i):
    return i - 1 if i % 2 == 0 else i + 1


def place_of(block, owner):
    offset = block - owner
    side = jnp.where(offset == 1 - 2 * lax.rem(owner, 2), PARTNER, DIAGONAL)
    away = jnp.where(offset == -REACH, BELOW, jnp.where(offset == REACH, ABOVE, side))
    return jnp.where(offset == 0, OWN, away)


def shifted(rows, amount):
    if amount == 0:
        return rows
    length = rows.shape[-1]
    moved = pltpu.roll(rows, amount % length, 1)
    edge = slice(0, LANES) if amount > 0 else slice(length - LANES, length)
    lane = lax.broadcasted_iota(jnp.int32, (rows.shape[0], LANES), 1)
    keep = lane >= amount if amount > 0 else lane < LANES + amount
    cut = jnp.where(keep, moved[:, edge], jnp.zeros((), rows.dtype))
    if amount > 0:
        return jnp.concatenate([cut, moved[:, LANES:]], axis=1)
    return jnp.concatenate([moved[:, : length - LANES], cut], axis=1)


def contract_lanes(left, right):
    return lax.dot_general(
        left, right, (((1,), (1,)), ((), ())), preferred_element_type=jnp.float32
    )


def make_band(taps_ref, band_ref):
    taps = taps_ref[...]
    wide = jnp.concatenate([taps, jnp.zeros((1, TILE - taps.shape[1]), jnp.float32)], axis=1)
    band = pltpu.roll(jnp.broadcast_to(wide, (TILE, TILE)), 0, 1, stride=1, stride_axis=0)
    row = lax.broadcasted_iota(jnp.int32, (TILE, TILE), 0)
    column = lax.broadcasted_iota(jnp.int32, (TILE, TILE), 1)
    band_ref[0] = jnp.where(column >= row, band, 0.0).astype(jnp.bfloat16)
    band_ref[1] = jnp.where(column < row, band, 0.0).astype(jnp.bfloat16)


def normalise(source_ref, band_ref, unit_ref, place, window):
    length = source_ref.shape[-1]
    pieces = []
    for start in range(0, length, TILE):
        piece = jnp.dot(
            source_ref[:, start : start + TILE], band_ref[0], preferred_element_type=jnp.float32
        )
        if start > 0:
            piece += jnp.dot(
                source_ref[:, start - TILE : start], band_ref[1],
                preferred_element_type=jnp.float32,
            )
        pieces.append(piece)
    filtered = jnp.concatenate(pieces, axis=1)
    meansq = jnp.mean(filtered * filtered, axis=-1, keepdims=True)
    unit_ref[place, :, window * length : (window + 1) * length] = (
        filtered * lax.rsqrt(meansq + 1e-06)
    ).astype(jnp.bfloat16)


def correlate(slot, scale, pairs_ref, count_ref, unit_ref, left_ref, right_ref, stage_ref,
              out_ref, sems):
    _, channels, both = unit_ref.shape
    half_rows = stage_ref.shape[1]
    length = both // 2
    owner = lax.axis_index("chan")
    first_row = pl.multiple_of(lax.axis_index("tm") * half_rows, half_rows)
    source = place_of(pairs_ref[0, slot], owner)
    partner = place_of(pairs_ref[1, slot], owner)
    factor = jnp.where(slot < count_ref[0], scale, 0.0)
    copies = []
    for sign in (1, -1):
        for window in range(2):
            span = slice(window * length, (window + 1) * length)
            rows = unit_ref[source, pl.ds(first_row, half_rows), span]
            for place in range(FINE + 1 if sign > 0 else FINE):
                step = place if sign > 0 else place - FINE
                left_ref[place * half_rows : (place + 1) * half_rows, span] = shifted(rows, step)
            rows = unit_ref[partner, :, span]
            for place in range(COARSE):
                right_ref[place * channels : (place + 1) * channels, span] = shifted(
                    rows, -sign * FINE * place
                )
        for pair in range(0, COARSE, 2):
            tall = FINE + 1 if sign > 0 and pair + 2 == COARSE else FINE
            result = contract_lanes(
                left_ref[: tall * half_rows, :],
                right_ref[pair * channels : (pair + 2) * channels, :],
            )
            lags = []
            for within in range(2):
                for place in range(tall):
                    if place == FINE and within == 0:
                        continue
                    coarse = sign * FINE * (pair + within)
                    lag = LAG + coarse + (place if sign > 0 else place - FINE)
                    stage_ref[lag] = factor * result[
                        place * half_rows : (place + 1) * half_rows,
                        within * channels : (within + 1) * channels,
                    ]
                    lags.append(lag)
            span = pl.ds(min(lags), len(lags))
            copy = pltpu.make_async_copy(
                stage_ref.at[span], out_ref.at[slot, span], sems.at[len(copies)]
            )
            copy.start()
            copies.append(copy)
    return copies


def early_kernel(taps_ref, *refs):
    blocks, (band_ref, unit_ref) = refs[:4], refs[4:]
    make_band(taps_ref, band_ref)
    for place in range(2):
        for window in range(2):
            normalise(blocks[2 * place + window], band_ref, unit_ref, OWN + place, window)


def stage_kernel(scale, slots, places, pairs_ref, count_ref, band_ref, *refs):
    blocks = refs[: 2 * len(places)]
    refs = refs[2 * len(places) :]
    refs = refs[1:] if len(slots) == 1 else refs[2:]
    unit_ref, out_ref, left_ref, right_ref, stage_ref, sems = refs
    for index, place in enumerate(places):
        for window in range(2):
            normalise(blocks[2 * index + window], band_ref, unit_ref, place, window)
    copies = []
    for index, slot in enumerate(slots):
        copies += correlate(
            slot, scale, pairs_ref, count_ref, unit_ref, left_ref, right_ref,
            stage_ref.at[index], out_ref, sems.at[index],
        )
    for copy in copies:
        copy.wait()


def body(traces, fir_taps, pair_blocks, pair_count):
    rows, windows, length = traces.shape
    block = traces.reshape(rows, length)
    halves = lax.axis_size("tm")
    cap = pair_blocks.shape[0]
    lags = 2 * LAG + 1
    half_rows = rows // halves
    scale = float(windows * halves * length) ** (-0.5)

    swap = lambda array: passed(array, "tm", lambda i: 1 - i)
    partner = passed(block, "chan", partner_of)
    below = passed(block, "chan", lambda i: i + REACH)
    above = passed(block, "chan", lambda i: i - REACH)
    diagonal = passed(block, "chan", diagonal_of)
    own, taps, pairs, count = lax.optimization_barrier(
        (block, fir_taps.astype(jnp.float32)[None, :], pair_blocks.T, pair_count)
    )

    smem = pl.BlockSpec(memory_space=pltpu.SMEM)
    vmem = pl.BlockSpec(memory_space=pltpu.VMEM)
    hbm = pl.BlockSpec(memory_space=pl.ANY)
    params = pltpu.CompilerParams(vmem_limit_bytes=40 * 1024 * 1024)
    band_shape = jax.ShapeDtypeStruct((2, TILE, TILE), jnp.bfloat16)
    unit_shape = jax.ShapeDtypeStruct((NEAR, rows, halves * length), jnp.bfloat16)
    out_shape = jax.ShapeDtypeStruct((cap, lags, half_rows, rows), jnp.float32)

    def cost(blocks, slots):
        return pl.CostEstimate(
            flops=blocks * 2 * 2 * rows * length * 2 * TILE
            + slots * 2 * lags * half_rows * rows * halves * length,
            bytes_accessed=slots * lags * half_rows * rows * 4,
            transcendentals=0,
        )

    def stage(slots, places, blocks, band, unit, out):
        aliased = [unit] if out is None else [unit, out]
        first = 3 + len(blocks)
        return pl.pallas_call(
            functools.partial(stage_kernel, scale, slots, places),
            out_shape=(unit_shape, out_shape),
            in_specs=[smem, smem, vmem] + [vmem] * len(blocks) + [vmem, hbm][: len(aliased)],
            out_specs=(vmem, hbm),
            input_output_aliases={first + i: i for i in range(len(aliased))},
            scratch_shapes=[
                pltpu.VMEM(((FINE + 1) * half_rows, halves * length), jnp.bfloat16),
                pltpu.VMEM((COARSE * rows, halves * length), jnp.bfloat16),
                pltpu.VMEM((len(slots), lags, half_rows, rows), jnp.float32),
                pltpu.SemaphoreType.DMA((len(slots), CHUNKS)),
            ],
            compiler_params=params,
            cost_estimate=cost(len(places), len(slots)),
        )(pairs, count, band, *blocks, *aliased)

    band, unit = pl.pallas_call(
        early_kernel,
        out_shape=(band_shape, unit_shape),
        in_specs=[vmem] * 5,
        out_specs=(vmem, vmem),
        compiler_params=params,
        cost_estimate=cost(2, 0),
    )(taps, own, swap(own), partner, swap(partner))
    unit, out = stage(
        (0,), (BELOW, ABOVE), (below, swap(below), above, swap(above)), band, unit, None
    )
    diagonal, unit = lax.optimization_barrier((diagonal, unit))
    unit, out = stage(
        tuple(range(1, cap)), (DIAGONAL,), (diagonal, swap(diagonal)), band, unit, out
    )
    return jnp.transpose(out, (0, 2, 1, 3))


def solution(mesh):
    return jax.shard_map(
        body,
        mesh=mesh,
        in_specs=(
            P(("groups", "chan"), "tm", None),
            P(),
            P(("groups", "chan"), None),
            P(("groups", "chan")),
        ),
        out_specs=P(("groups", "chan"), "tm", None, None),
        check_vma=False,
    )
```

```python
import functools

import jax
import jax.numpy as jnp
from jax import lax
from jax.experimental import pallas as pl
from jax.experimental.pallas import tpu as pltpu
from jax.sharding import PartitionSpec as P

LAG = 32
REACH = 2
NEAR = 2 * REACH + 1
FINE = 8
COARSE = LAG // FINE
LANES = 128
TILE = 256
CHUNKS = 4
OWN, PARTNER, BELOW, ABOVE, DIAGONAL = range(NEAR)


def passed(block, axis, target):
    size = lax.axis_size(axis)
    route = [(i, target(i)) for i in range(size) if 0 <= target(i) < size]
    return lax.ppermute(block, axis, route)


def partner_of(i):
    return i + 1 if i % 2 == 0 else i - 1


def diagonal_of(i):
    return i - 1 if i % 2 == 0 else i + 1


def place_of(block, owner):
    offset = block - owner
    side = jnp.where(offset == 1 - 2 * lax.rem(owner, 2), PARTNER, DIAGONAL)
    away = jnp.where(offset == -REACH, BELOW, jnp.where(offset == REACH, ABOVE, side))
    return jnp.where(offset == 0, OWN, away)


def shifted(rows, amount):
    if amount == 0:
        return rows
    length = rows.shape[-1]
    moved = pltpu.roll(rows, amount % length, 1)
    edge = slice(0, LANES) if amount > 0 else slice(length - LANES, length)
    lane = lax.broadcasted_iota(jnp.int32, (rows.shape[0], LANES), 1)
    keep = lane >= amount if amount > 0 else lane < LANES + amount
    cut = jnp.where(keep, moved[:, edge], jnp.zeros((), rows.dtype))
    if amount > 0:
        return jnp.concatenate([cut, moved[:, LANES:]], axis=1)
    return jnp.concatenate([moved[:, : length - LANES], cut], axis=1)


def contract_lanes(left, right):
    return lax.dot_general(
        left, right, (((1,), (1,)), ((), ())), preferred_element_type=jnp.float32
    )


def make_band(taps_ref, band_ref):
    taps = taps_ref[...]
    wide = jnp.concatenate([taps, jnp.zeros((1, TILE - taps.shape[1]), jnp.float32)], axis=1)
    band = pltpu.roll(jnp.broadcast_to(wide, (TILE, TILE)), 0, 1, stride=1, stride_axis=0)
    row = lax.broadcasted_iota(jnp.int32, (TILE, TILE), 0)
    column = lax.broadcasted_iota(jnp.int32, (TILE, TILE), 1)
    band_ref[0] = jnp.where(column >= row, band, 0.0).astype(jnp.bfloat16)
    band_ref[1] = jnp.where(column < row, band, 0.0).astype(jnp.bfloat16)


def normalise(source_ref, band_ref, unit_ref, place, window):
    rows, length = unit_ref.shape[1], source_ref.shape[-1]
    pieces = []
    for start in range(0, length, TILE):
        piece = jnp.dot(
            source_ref[:rows, start : start + TILE], band_ref[0], preferred_element_type=jnp.float32
        )
        if start > 0:
            piece += jnp.dot(
                source_ref[:rows, start - TILE : start], band_ref[1],
                preferred_element_type=jnp.float32,
            )
        pieces.append(piece)
    filtered = jnp.concatenate(pieces, axis=1)
    meansq = jnp.mean(filtered * filtered, axis=-1, keepdims=True)
    unit_ref[place, :, window * length : (window + 1) * length] = (
        filtered * lax.rsqrt(meansq + 1e-06)
    ).astype(jnp.bfloat16)


def prepare(slot, sign, pairs_ref, unit_ref, left_ref, right_ref, half_rows):
    _, channels, both = unit_ref.shape
    length = both // 2
    owner = lax.axis_index("chan")
    first_row = pl.multiple_of(lax.axis_index("tm") * half_rows, half_rows)
    source = place_of(pairs_ref[0, slot], owner)
    partner = place_of(pairs_ref[1, slot], owner)
    for window in range(2):
        span = slice(window * length, (window + 1) * length)
        rows = unit_ref[source, pl.ds(first_row, half_rows), span]
        for place in range(FINE + 1 if sign > 0 else FINE):
            step = place if sign > 0 else place - FINE
            left_ref[place * half_rows : (place + 1) * half_rows, span] = shifted(rows, step)
        rows = unit_ref[partner, :, span]
        for place in range(COARSE):
            right_ref[place * channels : (place + 1) * channels, span] = shifted(
                rows, -sign * FINE * place
            )


def correlate(slot, sign, pair, factor, left_ref, right_ref, stage_ref, out_ref, sem):
    half_rows, channels = stage_ref.shape[1:]
    tall = FINE + 1 if sign > 0 and pair + 2 == COARSE else FINE
    result = contract_lanes(
        left_ref[: tall * half_rows, :],
        right_ref[pair * channels : (pair + 2) * channels, :],
    )
    lags = []
    for within in range(2):
        for place in range(tall):
            if place == FINE and within == 0:
                continue
            coarse = sign * FINE * (pair + within)
            lag = LAG + coarse + (place if sign > 0 else place - FINE)
            stage_ref[lag] = factor * result[
                place * half_rows : (place + 1) * half_rows,
                within * channels : (within + 1) * channels,
            ]
            lags.append(lag)
    span = pl.ds(min(lags), len(lags))
    copy = pltpu.make_async_copy(stage_ref.at[span], out_ref.at[slot, span], sem)
    copy.start()
    return copy


def early_kernel(pairs_ref, count_ref, taps_ref, *refs):
    blocks, (band_ref, unit_ref) = refs[:2], refs[2:]
    make_band(taps_ref, band_ref)
    for window in range(2):
        normalise(blocks[window], band_ref, unit_ref, OWN, window)


def stage_kernel(scale, slots, places, pairs_ref, count_ref, band_ref, *refs):
    blocks = refs[: 2 * len(places)]
    refs = refs[2 * len(places) :]
    refs = refs[1:] if len(slots) == 1 else refs[2:]
    unit_ref, out_ref, left_ref, right_ref, stage_ref, sems = refs
    for index, place in enumerate(places):
        for window in range(2):
            normalise(blocks[2 * index + window], band_ref, unit_ref, place, window)
    steps = [(index, slot, sign) for index, slot in enumerate(slots) for sign in (1, -1)]

    def ready(number):
        if number < len(steps):
            _, slot, sign = steps[number]
            prepare(
                slot, sign, pairs_ref, unit_ref, left_ref.at[number % 2],
                right_ref.at[number % 2], stage_ref.shape[2],
            )

    copies = []
    ready(0)
    for number, (index, slot, sign) in enumerate(steps):
        ready(number + 1)
        factor = jnp.where(slot < count_ref[0], scale, 0.0)
        for pair in range(0, COARSE, 2):
            copies.append(
                correlate(
                    slot, sign, pair, factor, left_ref.at[number % 2], right_ref.at[number % 2],
                    stage_ref.at[index], out_ref, sems.at[index, len(copies) % CHUNKS],
                )
            )
    for copy in copies:
        copy.wait()


def body(traces, fir_taps, pair_blocks, pair_count):
    rows, windows, length = traces.shape
    block = traces.reshape(rows, length)
    halves = lax.axis_size("tm")
    cap = pair_blocks.shape[0]
    lags = 2 * LAG + 1
    half_rows = rows // halves
    scale = float(windows * halves * length) ** (-0.5)

    swap = lambda array: passed(array, "tm", lambda i: 1 - i)
    partner = passed(block, "chan", partner_of)
    below = passed(block, "chan", lambda i: i + REACH)
    above = passed(block, "chan", lambda i: i - REACH)
    padded = jnp.pad(block, ((0, 16), (0, 0)))
    diagonal = passed(padded, "chan", diagonal_of)
    own, pairs, count = block, pair_blocks.T, pair_count
    taps = fir_taps.astype(jnp.float32)[None, :]

    smem = pl.BlockSpec(memory_space=pltpu.SMEM)
    vmem = pl.BlockSpec(memory_space=pltpu.VMEM)
    hbm = pl.BlockSpec(memory_space=pl.ANY)
    params = pltpu.CompilerParams(vmem_limit_bytes=40 * 1024 * 1024)
    band_shape = jax.ShapeDtypeStruct((2, TILE, TILE), jnp.bfloat16)
    unit_shape = jax.ShapeDtypeStruct((NEAR, rows, halves * length), jnp.bfloat16)
    out_shape = jax.ShapeDtypeStruct((cap, lags, half_rows, rows), jnp.float32)

    light = pl.CostEstimate(flops=1, bytes_accessed=1, transcendentals=0)
    heavy = pl.CostEstimate(
        flops=2 * (cap - 1) * lags * half_rows * rows * halves * length,
        bytes_accessed=(cap - 1) * lags * half_rows * rows * 4,
        transcendentals=0,
    )

    def stage(slots, places, blocks, band, unit, out):
        aliased = [unit] if out is None else [unit, out]
        first = 3 + len(blocks)
        return pl.pallas_call(
            functools.partial(stage_kernel, scale, slots, places),
            out_shape=(unit_shape, out_shape),
            in_specs=[smem, smem, vmem] + [vmem] * len(blocks) + [vmem, hbm][: len(aliased)],
            out_specs=(vmem, hbm),
            input_output_aliases={first + i: i for i in range(len(aliased))},
            scratch_shapes=[
                pltpu.VMEM((2, (FINE + 1) * half_rows, halves * length), jnp.bfloat16),
                pltpu.VMEM((2, COARSE * rows, halves * length), jnp.bfloat16),
                pltpu.VMEM((len(slots), lags, half_rows, rows), jnp.float32),
                pltpu.SemaphoreType.DMA((len(slots), CHUNKS)),
            ],
            compiler_params=params,
            cost_estimate=light if out is None else heavy,
        )(pairs, count, band, *blocks, *aliased)

    band, unit = pl.pallas_call(
        early_kernel,
        out_shape=(band_shape, unit_shape),
        in_specs=[smem, smem] + [vmem] * 3,
        out_specs=(vmem, vmem),
        compiler_params=params,
        cost_estimate=light,
    )(pairs, count, taps, padded, swap(own))
    partner, band = lax.optimization_barrier((partner, band))
    unit, out = stage(
        (0,), (ABOVE, BELOW, PARTNER),
        (above, swap(above), below, swap(below), partner, swap(partner)), band, unit, None,
    )
    diagonal, unit = lax.optimization_barrier((diagonal, unit))
    unit, out = stage(
        tuple(range(1, cap)), (DIAGONAL,), (diagonal, swap(diagonal)), band, unit, out
    )
    return jnp.transpose(out, (0, 2, 1, 3))


def solution(mesh):
    return jax.shard_map(
        body,
        mesh=mesh,
        in_specs=(
            P(("groups", "chan"), "tm", None),
            P(),
            P(("groups", "chan"), None),
            P(("groups", "chan")),
        ),
        out_specs=P(("groups", "chan"), "tm", None, None),
        check_vma=False,
    )
```

```python
import functools

import jax
import jax.numpy as jnp
from jax import lax
from jax.experimental import pallas as pl
from jax.experimental.pallas import tpu as pltpu
from jax.sharding import PartitionSpec as P

LAG = 32
REACH = 2
NEAR = 2 * REACH + 1
FINE = 8
COARSE = LAG // FINE
LANES = 128
TILE = 256
CHUNKS = 4
MARGIN = 32
OWN, PARTNER, BELOW, ABOVE, DIAGONAL = range(NEAR)


def passed(block, axis, target):
    size = lax.axis_size(axis)
    route = [(i, target(i)) for i in range(size) if 0 <= target(i) < size]
    return lax.ppermute(block, axis, route)


def partner_of(i):
    return i + 1 if i % 2 == 0 else i - 1


def diagonal_of(i):
    return i - 1 if i % 2 == 0 else i + 1


def place_of(block, owner):
    offset = block - owner
    side = jnp.where(offset == 1 - 2 * lax.rem(owner, 2), PARTNER, DIAGONAL)
    away = jnp.where(offset == -REACH, BELOW, jnp.where(offset == REACH, ABOVE, side))
    return jnp.where(offset == 0, OWN, away)


def shifted(rows, amount):
    if amount == 0:
        return rows
    length = rows.shape[-1]
    moved = pltpu.roll(rows, amount % length, 1)
    edge = slice(0, LANES) if amount > 0 else slice(length - LANES, length)
    lane = lax.broadcasted_iota(jnp.int32, (rows.shape[0], LANES), 1)
    keep = lane >= amount if amount > 0 else lane < LANES + amount
    cut = jnp.where(keep, moved[:, edge], jnp.zeros((), rows.dtype))
    if amount > 0:
        return jnp.concatenate([cut, moved[:, LANES:]], axis=1)
    return jnp.concatenate([moved[:, : length - LANES], cut], axis=1)


def make_band(taps_ref, band_ref):
    taps = taps_ref[...]
    wide = jnp.concatenate([taps, jnp.zeros((1, TILE - taps.shape[1]), jnp.float32)], axis=1)
    band = pltpu.roll(jnp.broadcast_to(wide, (TILE, TILE)), 0, 1, stride=1, stride_axis=0)
    row = lax.broadcasted_iota(jnp.int32, (TILE, TILE), 0)
    column = lax.broadcasted_iota(jnp.int32, (TILE, TILE), 1)
    band_ref[0] = jnp.where(column >= row, band, 0.0).astype(jnp.bfloat16)
    band_ref[1] = jnp.where(column < row, band, 0.0).astype(jnp.bfloat16)


def normalise(source_ref, band_ref, unit_ref, tall_ref, place, window):
    rows, length = unit_ref.shape[1], source_ref.shape[-1]
    pieces = []
    for start in range(0, length, TILE):
        piece = jnp.dot(
            source_ref[:rows, start : start + TILE], band_ref[0], preferred_element_type=jnp.float32
        )
        if start > 0:
            piece += jnp.dot(
                source_ref[:rows, start - TILE : start], band_ref[1],
                preferred_element_type=jnp.float32,
            )
        pieces.append(piece)
    filtered = jnp.concatenate(pieces, axis=1)
    meansq = jnp.mean(filtered * filtered, axis=-1, keepdims=True)
    unit = filtered * lax.rsqrt(meansq + 1e-06)
    unit_ref[place, :, window * length : (window + 1) * length] = unit.astype(jnp.bfloat16)
    tall = unit.T
    gap = jnp.zeros((FINE, rows), jnp.float32)
    edge = jnp.zeros((MARGIN, rows), jnp.bfloat16)
    inner = MARGIN - 2 * FINE
    for phase in range(2):
        tall_ref[place, window, phase, :MARGIN] = edge
        tall_ref[place, window, phase, length + MARGIN :] = edge
    tall_ref[place, window, 0, MARGIN : MARGIN + length] = tall.astype(jnp.bfloat16)
    tall_ref[place, window, 1, inner : inner + length + 2 * FINE] = jnp.concatenate(
        [gap, tall, gap], axis=0
    ).astype(jnp.bfloat16)


def prepare(source, sign, unit_ref, left_ref, half_rows):
    length = unit_ref.shape[2] // 2
    first_row = pl.multiple_of(lax.axis_index("tm") * half_rows, half_rows)
    for window in range(2):
        span = slice(window * length, (window + 1) * length)
        rows = unit_ref[source, pl.ds(first_row, half_rows), span]
        for place in range(FINE + 1 if sign > 0 else FINE):
            step = place if sign > 0 else place - FINE
            left_ref[place * half_rows : (place + 1) * half_rows, span] = shifted(rows, step)


def coarse_rows(tall_ref, partner, window, amount):
    length = tall_ref.shape[3] - 2 * MARGIN
    phase = amount // FINE % 2
    first = MARGIN + amount - FINE * phase
    return tall_ref[partner, window, phase, first : first + length]


def correlate(slot, sign, pair, factor, partner, left_ref, tall_ref, stage_ref, out_ref, sem):
    half_rows, channels = stage_ref.shape[1:]
    tall = FINE + 1 if sign > 0 and pair + 2 == COARSE else FINE
    right = jnp.concatenate(
        [
            jnp.concatenate(
                [
                    coarse_rows(tall_ref, partner, window, sign * FINE * (pair + within))
                    for within in range(2)
                ],
                axis=1,
            )
            for window in range(2)
        ],
        axis=0,
    )
    result = jnp.dot(
        left_ref[: tall * half_rows, :], right, preferred_element_type=jnp.float32
    )
    lags = []
    for within in range(2):
        for place in range(tall):
            if place == FINE and within == 0:
                continue
            coarse = sign * FINE * (pair + within)
            lag = LAG + coarse + (place if sign > 0 else place - FINE)
            stage_ref[lag] = factor * result[
                place * half_rows : (place + 1) * half_rows,
                within * channels : (within + 1) * channels,
            ]
            lags.append(lag)
    span = pl.ds(min(lags), len(lags))
    copy = pltpu.make_async_copy(stage_ref.at[span], out_ref.at[slot, span], sem)
    copy.start()
    return copy


def early_kernel(pairs_ref, count_ref, taps_ref, *refs):
    blocks, (band_ref, unit_ref, tall_ref) = refs[:2], refs[2:]
    make_band(taps_ref, band_ref)
    for window in range(2):
        normalise(blocks[window], band_ref, unit_ref, tall_ref, OWN, window)


def stage_kernel(scale, slots, places, pairs_ref, count_ref, band_ref, *refs):
    blocks = refs[: 2 * len(places)]
    refs = refs[2 * len(places) :]
    refs = refs[2:] if len(slots) == 1 else refs[3:]
    unit_ref, tall_ref, out_ref, left_ref, stage_ref, sems = refs
    for index, place in enumerate(places):
        for window in range(2):
            normalise(
                blocks[2 * index + window], band_ref, unit_ref, tall_ref, place, window
            )
    steps = [(index, slot, sign) for index, slot in enumerate(slots) for sign in (1, -1)]

    owner = lax.axis_index("chan")

    def ready(number):
        if number < len(steps):
            _, slot, sign = steps[number]
            source = place_of(pairs_ref[0, slot], owner)
            prepare(source, sign, unit_ref, left_ref.at[number % 2], stage_ref.shape[2])

    copies = []
    ready(0)
    for number, (index, slot, sign) in enumerate(steps):
        ready(number + 1)
        factor = jnp.where(slot < count_ref[0], scale, 0.0)
        partner = place_of(pairs_ref[1, slot], owner)
        for pair in range(0, COARSE, 2):
            copies.append(
                correlate(
                    slot, sign, pair, factor, partner, left_ref.at[number % 2], tall_ref,
                    stage_ref.at[index], out_ref, sems.at[index, len(copies) % CHUNKS],
                )
            )
    for copy in copies:
        copy.wait()


def body(traces, fir_taps, pair_blocks, pair_count):
    rows, windows, length = traces.shape
    block = traces.reshape(rows, length)
    halves = lax.axis_size("tm")
    cap = pair_blocks.shape[0]
    lags = 2 * LAG + 1
    half_rows = rows // halves
    scale = float(windows * halves * length) ** (-0.5)

    swap = lambda array: passed(array, "tm", lambda i: 1 - i)
    partner = passed(block, "chan", partner_of)
    below = passed(block, "chan", lambda i: i + REACH)
    above = passed(block, "chan", lambda i: i - REACH)
    padded = jnp.pad(block, ((0, 16), (0, 0)))
    own, pairs, count = block, pair_blocks.T, pair_count
    taps = fir_taps.astype(jnp.float32)[None, :]

    smem = pl.BlockSpec(memory_space=pltpu.SMEM)
    vmem = pl.BlockSpec(memory_space=pltpu.VMEM)
    hbm = pl.BlockSpec(memory_space=pl.ANY)
    params = pltpu.CompilerParams(vmem_limit_bytes=32 * 1024 * 1024)
    band_shape = jax.ShapeDtypeStruct((2, TILE, TILE), jnp.bfloat16)
    unit_shape = jax.ShapeDtypeStruct((NEAR, rows, halves * length), jnp.bfloat16)
    tall_shape = jax.ShapeDtypeStruct(
        (NEAR, halves, 2, length + 2 * MARGIN, rows), jnp.bfloat16
    )
    out_shape = jax.ShapeDtypeStruct((cap, lags, half_rows, rows), jnp.float32)

    light = pl.CostEstimate(flops=1, bytes_accessed=1, transcendentals=0)
    heavy = pl.CostEstimate(
        flops=2 * (cap - 1) * lags * half_rows * rows * halves * length,
        bytes_accessed=(cap - 1) * lags * half_rows * rows * 4,
        transcendentals=0,
    )

    def stage(slots, places, blocks, band, unit, tall, out):
        aliased = [unit, tall] if out is None else [unit, tall, out]
        first = 3 + len(blocks)
        return pl.pallas_call(
            functools.partial(stage_kernel, scale, slots, places),
            out_shape=(unit_shape, tall_shape, out_shape),
            in_specs=[smem, smem, vmem] + [vmem] * len(blocks) + [vmem, vmem, hbm][: len(aliased)],
            out_specs=(vmem, vmem, hbm),
            input_output_aliases={first + i: i for i in range(len(aliased))},
            scratch_shapes=[
                pltpu.VMEM((2, (FINE + 1) * half_rows, halves * length), jnp.bfloat16),
                pltpu.VMEM((len(slots), lags, half_rows, rows), jnp.float32),
                pltpu.SemaphoreType.DMA((len(slots), CHUNKS)),
            ],
            compiler_params=params,
            cost_estimate=light if out is None else heavy,
        )(pairs, count, band, *blocks, *aliased)

    band, unit, tall = pl.pallas_call(
        early_kernel,
        out_shape=(band_shape, unit_shape, tall_shape),
        in_specs=[smem, smem] + [vmem] * 3,
        out_specs=(vmem, vmem, vmem),
        compiler_params=params,
        cost_estimate=light,
    )(pairs, count, taps, padded, swap(own))
    sent, band = lax.optimization_barrier((padded, band))
    diagonal = passed(sent, "chan", diagonal_of)
    unit, tall, out = stage(
        (0,), (ABOVE, BELOW, PARTNER),
        (above, swap(above), below, swap(below), partner, swap(partner)), band, unit, tall, None,
    )
    diagonal, unit = lax.optimization_barrier((diagonal, unit))
    unit, tall, out = stage(
        tuple(range(1, cap)), (DIAGONAL,), (diagonal, swap(diagonal)), band, unit, tall, out
    )
    return jnp.transpose(out, (0, 2, 1, 3))


def solution(mesh):
    return jax.shard_map(
        body,
        mesh=mesh,
        in_specs=(
            P(("groups", "chan"), "tm", None),
            P(),
            P(("groups", "chan"), None),
            P(("groups", "chan")),
        ),
        out_specs=P(("groups", "chan"), "tm", None, None),
        check_vma=False,
    )
```

```python
import functools

import jax
import jax.numpy as jnp
from jax import lax
from jax.experimental import pallas as pl
from jax.experimental.pallas import tpu as pltpu
from jax.sharding import PartitionSpec as P

LAG = 32
REACH = 2
NEAR = 2 * REACH + 1
FINE = 8
COARSE = LAG // FINE
LANES = 128
TILE = 256
MARGIN = 32
OWN, PARTNER, BELOW, ABOVE, DIAGONAL = range(NEAR)


def passed(block, axis, target):
    size = lax.axis_size(axis)
    route = [(i, target(i)) for i in range(size) if 0 <= target(i) < size]
    return lax.ppermute(block, axis, route)


def partner_of(i):
    return i + 1 if i % 2 == 0 else i - 1


def diagonal_of(i):
    return i - 1 if i % 2 == 0 else i + 1


def place_of(block, owner):
    offset = block - owner
    side = jnp.where(offset == 1 - 2 * lax.rem(owner, 2), PARTNER, DIAGONAL)
    away = jnp.where(offset == -REACH, BELOW, jnp.where(offset == REACH, ABOVE, side))
    return jnp.where(offset == 0, OWN, away)


def shifted(rows, amount):
    if amount == 0:
        return rows
    length = rows.shape[-1]
    moved = pltpu.roll(rows, amount % length, 1)
    edge = slice(0, LANES) if amount > 0 else slice(length - LANES, length)
    lane = lax.broadcasted_iota(jnp.int32, (rows.shape[0], LANES), 1)
    keep = lane >= amount if amount > 0 else lane < LANES + amount
    cut = jnp.where(keep, moved[:, edge], jnp.zeros((), rows.dtype))
    if amount > 0:
        return jnp.concatenate([cut, moved[:, LANES:]], axis=1)
    return jnp.concatenate([moved[:, : length - LANES], cut], axis=1)


def make_band(taps_ref, band_ref):
    taps = taps_ref[...]
    wide = jnp.concatenate([taps, jnp.zeros((1, TILE - taps.shape[1]), jnp.float32)], axis=1)
    band = pltpu.roll(jnp.broadcast_to(wide, (TILE, TILE)), 0, 1, stride=1, stride_axis=0)
    row = lax.broadcasted_iota(jnp.int32, (TILE, TILE), 0)
    column = lax.broadcasted_iota(jnp.int32, (TILE, TILE), 1)
    band_ref[0] = jnp.where(column >= row, band, 0.0).astype(jnp.bfloat16)
    band_ref[1] = jnp.where(column < row, band, 0.0).astype(jnp.bfloat16)


def normalise(source_ref, band_ref, unit_ref, tall_ref, place, window):
    rows, length = unit_ref.shape[1], source_ref.shape[-1]
    pieces = []
    for start in range(0, length, TILE):
        piece = jnp.dot(
            source_ref[:rows, start : start + TILE], band_ref[0], preferred_element_type=jnp.float32
        )
        if start > 0:
            piece += jnp.dot(
                source_ref[:rows, start - TILE : start], band_ref[1],
                preferred_element_type=jnp.float32,
            )
        pieces.append(piece)
    filtered = jnp.concatenate(pieces, axis=1)
    meansq = jnp.mean(filtered * filtered, axis=-1, keepdims=True)
    unit = filtered * lax.rsqrt(meansq + 1e-06)
    unit_ref[place, :, window * length : (window + 1) * length] = unit.astype(jnp.bfloat16)
    tall = unit.T
    gap = jnp.zeros((FINE, rows), jnp.float32)
    edge = jnp.zeros((MARGIN, rows), jnp.bfloat16)
    inner = MARGIN - 2 * FINE
    for phase in range(2):
        tall_ref[place, window, phase, :MARGIN] = edge
        tall_ref[place, window, phase, length + MARGIN :] = edge
    tall_ref[place, window, 0, MARGIN : MARGIN + length] = tall.astype(jnp.bfloat16)
    tall_ref[place, window, 1, inner : inner + length + 2 * FINE] = jnp.concatenate(
        [gap, tall, gap], axis=0
    ).astype(jnp.bfloat16)


def prepare(source, sign, unit_ref, left_ref, half_rows):
    length = unit_ref.shape[2] // 2
    first_row = pl.multiple_of(lax.axis_index("tm") * half_rows, half_rows)
    for window in range(2):
        span = slice(window * length, (window + 1) * length)
        rows = unit_ref[source, pl.ds(first_row, half_rows), span]
        for place in range(FINE + 1 if sign > 0 else FINE):
            step = place if sign > 0 else place - FINE
            left_ref[place * half_rows : (place + 1) * half_rows, span] = shifted(rows, step)


def coarse_rows(tall_ref, partner, window, amount):
    length = tall_ref.shape[3] - 2 * MARGIN
    phase = amount // FINE % 2
    first = MARGIN + amount - FINE * phase
    return tall_ref[partner, window, phase, first : first + length]


def coarse_columns(tall_ref, partner, amounts):
    return jnp.concatenate(
        [
            jnp.concatenate(
                [coarse_rows(tall_ref, partner, window, amount) for amount in amounts], axis=1
            )
            for window in range(2)
        ],
        axis=0,
    )


def correlate(slot, sign, factor, partner, left_ref, tall_ref, stage_ref, out_ref, sem):
    half_rows, channels = stage_ref.shape[1:]
    amounts = [sign * FINE * place for place in range(COARSE)]
    lags = []

    def keep(result, base, steps, amounts):
        for column, amount in enumerate(amounts):
            for row, step in enumerate(steps):
                stage_ref[base + amount + step] = factor * result[
                    row * half_rows : (row + 1) * half_rows,
                    column * channels : (column + 1) * channels,
                ]
                lags.append(base + amount + step)

    result = jnp.dot(
        left_ref[: FINE * half_rows, :], coarse_columns(tall_ref, partner, amounts),
        preferred_element_type=jnp.float32,
    )
    keep(result, LAG, range(FINE) if sign > 0 else range(-FINE, 0), amounts)
    if sign > 0:
        result = jnp.dot(
            left_ref[FINE * half_rows :, :], coarse_columns(tall_ref, partner, amounts[-1:]),
            preferred_element_type=jnp.float32,
        )
        keep(result, LAG, [FINE], amounts[-1:])
    span = pl.ds(min(lags), len(lags))
    copy = pltpu.make_async_copy(stage_ref.at[span], out_ref.at[slot, span], sem)
    copy.start()
    return copy


def early_kernel(pairs_ref, count_ref, taps_ref, *refs):
    blocks, (band_ref, unit_ref, tall_ref) = refs[:2], refs[2:]
    make_band(taps_ref, band_ref)
    for window in range(2):
        normalise(blocks[window], band_ref, unit_ref, tall_ref, OWN, window)


def filter_kernel(units, band_ref, *refs):
    blocks, (unit_ref, tall_ref) = refs[: len(units)], refs[len(units) + 2 :]
    for block, (place, window) in zip(blocks, units):
        normalise(block, band_ref, unit_ref, tall_ref, place, window)


def stack_kernel(scale, units, pairs_ref, count_ref, band_ref, *refs):
    blocks, refs = refs[: len(units)], refs[len(units) + 2 :]
    unit_ref, tall_ref, out_ref, left_ref, stage_ref, sems = refs
    for block, (place, window) in zip(blocks, units):
        normalise(block, band_ref, unit_ref, tall_ref, place, window)
    slots = out_ref.shape[0]
    steps = [(slot, sign) for slot in range(slots) for sign in (1, -1)]
    owner = lax.axis_index("chan")

    def ready(number):
        if number < len(steps):
            slot, sign = steps[number]
            source = place_of(pairs_ref[0, slot], owner)
            prepare(source, sign, unit_ref, left_ref.at[number % 2], stage_ref.shape[2])

    copies = []
    ready(0)
    for number, (slot, sign) in enumerate(steps):
        ready(number + 1)
        factor = jnp.where(slot < count_ref[0], scale, 0.0)
        partner = place_of(pairs_ref[1, slot], owner)
        copies.append(
            correlate(
                slot, sign, factor, partner, left_ref.at[number % 2], tall_ref,
                stage_ref.at[slot], out_ref, sems.at[number],
            )
        )
    for copy in copies:
        copy.wait()


def body(traces, fir_taps, pair_blocks, pair_count):
    rows, windows, length = traces.shape
    own = traces.reshape(rows, length)
    halves = lax.axis_size("tm")
    cap = pair_blocks.shape[0]
    lags = 2 * LAG + 1
    half_rows = rows // halves
    scale = float(windows * halves * length) ** (-0.5)

    swap = lambda array: passed(array, "tm", lambda i: 1 - i)
    partner = passed(own, "chan", partner_of)
    below = passed(own, "chan", lambda i: i + REACH)
    above = passed(own, "chan", lambda i: i - REACH)
    diagonal = passed(own, "chan", diagonal_of)
    pairs, count = pair_blocks.T, pair_count
    taps = fir_taps.astype(jnp.float32)[None, :]

    smem = pl.BlockSpec(memory_space=pltpu.SMEM)
    vmem = pl.BlockSpec(memory_space=pltpu.VMEM)
    hbm = pl.BlockSpec(memory_space=pl.ANY)
    params = pltpu.CompilerParams(vmem_limit_bytes=32 * 1024 * 1024)
    band_shape = jax.ShapeDtypeStruct((2, TILE, TILE), jnp.bfloat16)
    unit_shape = jax.ShapeDtypeStruct((NEAR, rows, halves * length), jnp.bfloat16)
    tall_shape = jax.ShapeDtypeStruct(
        (NEAR, halves, 2, length + 2 * MARGIN, rows), jnp.bfloat16
    )
    out_shape = jax.ShapeDtypeStruct((cap, lags, half_rows, rows), jnp.float32)
    light = pl.CostEstimate(flops=1, bytes_accessed=1, transcendentals=0)
    heavy = pl.CostEstimate(
        flops=2 * cap * lags * half_rows * rows * halves * length,
        bytes_accessed=cap * lags * half_rows * rows * 4,
        transcendentals=0,
    )

    band, unit, tall = pl.pallas_call(
        early_kernel,
        out_shape=(band_shape, unit_shape, tall_shape),
        in_specs=[smem, smem] + [vmem] * 3,
        out_specs=(vmem, vmem, vmem),
        compiler_params=params,
        cost_estimate=light,
    )(pairs, count, taps, own, swap(own))

    def more(units, blocks, unit, tall):
        return pl.pallas_call(
            functools.partial(filter_kernel, units),
            out_shape=(unit_shape, tall_shape),
            in_specs=[vmem] * (len(units) + 3),
            out_specs=(vmem, vmem),
            input_output_aliases={len(units) + 1: 0, len(units) + 2: 1},
            compiler_params=params,
            cost_estimate=light,
        )(band, *blocks, unit, tall)

    mine, other = 0, 1
    diagonal, band = lax.optimization_barrier((diagonal, band))
    unit, tall = more(
        ((DIAGONAL, mine), (DIAGONAL, other)), (diagonal, swap(diagonal)), unit, tall
    )
    unit, tall = more(
        ((ABOVE, mine), (BELOW, mine), (PARTNER, mine)), (above, below, partner), unit, tall
    )
    units = ((ABOVE, other), (BELOW, other), (PARTNER, other))
    _, _, out = pl.pallas_call(
        functools.partial(stack_kernel, scale, units),
        out_shape=(unit_shape, tall_shape, out_shape),
        in_specs=[smem, smem] + [vmem] * (len(units) + 3),
        out_specs=(vmem, vmem, hbm),
        input_output_aliases={len(units) + 3: 0, len(units) + 4: 1},
        scratch_shapes=[
            pltpu.VMEM((2, (FINE + 1) * half_rows, halves * length), jnp.bfloat16),
            pltpu.VMEM((cap, lags, half_rows, rows), jnp.float32),
            pltpu.SemaphoreType.DMA((2 * cap,)),
        ],
        compiler_params=params,
        cost_estimate=heavy,
    )(pairs, count, band, swap(above), swap(below), swap(partner), unit, tall)
    return jnp.transpose(out, (0, 2, 1, 3))


def solution(mesh):
    return jax.shard_map(
        body,
        mesh=mesh,
        in_specs=(
            P(("groups", "chan"), "tm", None),
            P(),
            P(("groups", "chan"), None),
            P(("groups", "chan")),
        ),
        out_specs=P(("groups", "chan"), "tm", None, None),
        check_vma=False,
    )
```

```python
import functools

import jax
import jax.numpy as jnp
from jax import lax
from jax.experimental import pallas as pl
from jax.experimental.pallas import tpu as pltpu
from jax.sharding import PartitionSpec as P

LAG = 32
REACH = 2
NEAR = 2 * REACH + 1
FINE = 8
COARSE = LAG // FINE
LANES = 128
TILE = 256
MARGIN = 32
OWN, PARTNER, BELOW, ABOVE, DIAGONAL = range(NEAR)


def passed(block, axis, target):
    size = lax.axis_size(axis)
    route = [(i, target(i)) for i in range(size) if 0 <= target(i) < size]
    return lax.ppermute(block, axis, route)


def partner_of(i):
    return i + 1 if i % 2 == 0 else i - 1


def diagonal_of(i):
    return i - 1 if i % 2 == 0 else i + 1


def place_of(block, owner):
    offset = block - owner
    side = jnp.where(offset == 1 - 2 * lax.rem(owner, 2), PARTNER, DIAGONAL)
    away = jnp.where(offset == -REACH, BELOW, jnp.where(offset == REACH, ABOVE, side))
    return jnp.where(offset == 0, OWN, away)


def shifted(rows, amount):
    if amount == 0:
        return rows
    length = rows.shape[-1]
    moved = pltpu.roll(rows, amount % length, 1)
    edge = slice(0, LANES) if amount > 0 else slice(length - LANES, length)
    lane = lax.broadcasted_iota(jnp.int32, (rows.shape[0], LANES), 1)
    keep = lane >= amount if amount > 0 else lane < LANES + amount
    cut = jnp.where(keep, moved[:, edge], jnp.zeros((), rows.dtype))
    if amount > 0:
        return jnp.concatenate([cut, moved[:, LANES:]], axis=1)
    return jnp.concatenate([moved[:, : length - LANES], cut], axis=1)


def make_band(taps_ref, band_ref):
    taps = taps_ref[...]
    wide = jnp.concatenate([taps, jnp.zeros((1, TILE - taps.shape[1]), jnp.float32)], axis=1)
    band = pltpu.roll(jnp.broadcast_to(wide, (TILE, TILE)), 0, 1, stride=1, stride_axis=0)
    row = lax.broadcasted_iota(jnp.int32, (TILE, TILE), 0)
    column = lax.broadcasted_iota(jnp.int32, (TILE, TILE), 1)
    band_ref[0] = jnp.where(column >= row, band, 0.0).astype(jnp.bfloat16)
    band_ref[1] = jnp.where(column < row, band, 0.0).astype(jnp.bfloat16)


def normalise(source_ref, band_ref, unit_ref, tall_ref, place, window):
    rows, length = unit_ref.shape[1], source_ref.shape[-1]
    tiles = length // TILE
    stacked = jnp.concatenate(
        [source_ref[:rows, tile * TILE : (tile + 1) * TILE] for tile in range(tiles)], axis=0
    )
    here = jnp.dot(stacked, band_ref[0], preferred_element_type=jnp.float32)
    after = jnp.dot(stacked[:-rows], band_ref[1], preferred_element_type=jnp.float32)
    pieces = [here[:rows]] + [
        here[tile * rows : (tile + 1) * rows] + after[(tile - 1) * rows : tile * rows]
        for tile in range(1, tiles)
    ]
    filtered = jnp.concatenate(pieces, axis=1)
    meansq = jnp.mean(filtered * filtered, axis=-1, keepdims=True)
    unit = filtered * lax.rsqrt(meansq + 1e-06)
    unit_ref[place, :, window * length : (window + 1) * length] = unit.astype(jnp.bfloat16)
    tall = unit.T
    gap = jnp.zeros((FINE, rows), jnp.float32)
    edge = jnp.zeros((MARGIN, rows), jnp.bfloat16)
    inner = MARGIN - 2 * FINE
    for phase in range(2):
        tall_ref[place, window, phase, :MARGIN] = edge
        tall_ref[place, window, phase, length + MARGIN :] = edge
    tall_ref[place, window, 0, MARGIN : MARGIN + length] = tall.astype(jnp.bfloat16)
    tall_ref[place, window, 1, inner : inner + length + 2 * FINE] = jnp.concatenate(
        [gap, tall, gap], axis=0
    ).astype(jnp.bfloat16)


def prepare(source, sign, unit_ref, left_ref, half_rows):
    length = unit_ref.shape[2] // 2
    first_row = pl.multiple_of(lax.axis_index("tm") * half_rows, half_rows)
    for window in range(2):
        span = slice(window * length, (window + 1) * length)
        rows = unit_ref[source, pl.ds(first_row, half_rows), span]
        for place in range(FINE + 1 if sign > 0 else FINE):
            step = place if sign > 0 else place - FINE
            left_ref[place * half_rows : (place + 1) * half_rows, span] = shifted(rows, step)


def coarse_rows(tall_ref, partner, window, amount):
    length = tall_ref.shape[3] - 2 * MARGIN
    phase = amount // FINE % 2
    first = MARGIN + amount - FINE * phase
    return tall_ref[partner, window, phase, first : first + length]


def coarse_columns(tall_ref, partner, amounts):
    return jnp.concatenate(
        [
            jnp.concatenate(
                [coarse_rows(tall_ref, partner, window, amount) for amount in amounts], axis=1
            )
            for window in range(2)
        ],
        axis=0,
    )


def correlate(slot, sign, factor, partner, left_ref, tall_ref, stage_ref, out_ref, sem):
    half_rows, channels = stage_ref.shape[1:]
    amounts = [sign * FINE * place for place in range(COARSE)]
    steps = list(range(FINE + 1) if sign > 0 else range(-FINE, 0))
    result = jnp.dot(
        left_ref[: len(steps) * half_rows, :], coarse_columns(tall_ref, partner, amounts),
        preferred_element_type=jnp.float32,
    )
    lags = []
    for column, amount in enumerate(amounts):
        for row, step in enumerate(steps):
            if step == FINE and column < COARSE - 1:
                continue
            lags.append(LAG + amount + step)
            stage_ref[lags[-1]] = factor * result[
                row * half_rows : (row + 1) * half_rows,
                column * channels : (column + 1) * channels,
            ]
    span = pl.ds(min(lags), len(lags))
    copy = pltpu.make_async_copy(stage_ref.at[span], out_ref.at[slot, span], sem)
    copy.start()
    return copy


def early_kernel(pairs_ref, count_ref, taps_ref, *refs):
    blocks, (band_ref, unit_ref, tall_ref) = refs[:3], refs[3:]
    make_band(taps_ref, band_ref)
    for block, (place, window) in zip(blocks, ((OWN, 0), (OWN, 1), (DIAGONAL, 0))):
        normalise(block, band_ref, unit_ref, tall_ref, place, window)


def filter_kernel(units, band_ref, *refs):
    blocks, (unit_ref, tall_ref) = refs[: len(units)], refs[len(units) + 2 :]
    for block, (place, window) in zip(blocks, units):
        normalise(block, band_ref, unit_ref, tall_ref, place, window)


def stack_kernel(scale, units, pairs_ref, count_ref, band_ref, *refs):
    blocks, refs = refs[: len(units)], refs[len(units) + 2 :]
    unit_ref, tall_ref, out_ref, left_ref, stage_ref, sems = refs
    for block, (place, window) in zip(blocks, units):
        normalise(block, band_ref, unit_ref, tall_ref, place, window)
    slots = out_ref.shape[0]
    steps = [(slot, sign) for slot in range(slots) for sign in (1, -1)]
    owner = lax.axis_index("chan")

    def ready(number):
        if number < len(steps):
            slot, sign = steps[number]
            source = place_of(pairs_ref[0, slot], owner)
            prepare(source, sign, unit_ref, left_ref.at[number % 2], stage_ref.shape[2])

    copies = []
    ready(0)
    for number, (slot, sign) in enumerate(steps):
        ready(number + 1)
        factor = jnp.where(slot < count_ref[0], scale, 0.0)
        partner = place_of(pairs_ref[1, slot], owner)
        copies.append(
            correlate(
                slot, sign, factor, partner, left_ref.at[number % 2], tall_ref,
                stage_ref.at[slot], out_ref, sems.at[number],
            )
        )
    for copy in copies:
        copy.wait()


def body(traces, fir_taps, pair_blocks, pair_count):
    rows, windows, length = traces.shape
    own = traces.reshape(rows, length)
    halves = lax.axis_size("tm")
    cap = pair_blocks.shape[0]
    lags = 2 * LAG + 1
    half_rows = rows // halves
    scale = float(windows * halves * length) ** (-0.5)

    swap = lambda array: passed(array, "tm", lambda i: 1 - i)
    partner = passed(own, "chan", partner_of)
    below = passed(own, "chan", lambda i: i + REACH)
    above = passed(own, "chan", lambda i: i - REACH)
    diagonal = passed(own, "chan", diagonal_of)
    pairs, count = pair_blocks.T, pair_count
    taps = fir_taps.astype(jnp.float32)[None, :]

    smem = pl.BlockSpec(memory_space=pltpu.SMEM)
    vmem = pl.BlockSpec(memory_space=pltpu.VMEM)
    hbm = pl.BlockSpec(memory_space=pl.ANY)
    params = pltpu.CompilerParams(vmem_limit_bytes=32 * 1024 * 1024)
    band_shape = jax.ShapeDtypeStruct((2, TILE, TILE), jnp.bfloat16)
    unit_shape = jax.ShapeDtypeStruct((NEAR, rows, halves * length), jnp.bfloat16)
    tall_shape = jax.ShapeDtypeStruct(
        (NEAR, halves, 2, length + 2 * MARGIN, rows), jnp.bfloat16
    )
    out_shape = jax.ShapeDtypeStruct((cap, lags, half_rows, rows), jnp.float32)
    light = pl.CostEstimate(flops=1, bytes_accessed=1, transcendentals=0)
    heavy = pl.CostEstimate(
        flops=2 * cap * lags * half_rows * rows * halves * length,
        bytes_accessed=cap * lags * half_rows * rows * 4,
        transcendentals=0,
    )

    band, unit, tall = pl.pallas_call(
        early_kernel,
        out_shape=(band_shape, unit_shape, tall_shape),
        in_specs=[smem, smem] + [vmem] * 4,
        out_specs=(vmem, vmem, vmem),
        compiler_params=params,
        cost_estimate=light,
    )(pairs, count, taps, own, swap(own), diagonal)

    def more(units, blocks, unit, tall):
        return pl.pallas_call(
            functools.partial(filter_kernel, units),
            out_shape=(unit_shape, tall_shape),
            in_specs=[vmem] * (len(units) + 3),
            out_specs=(vmem, vmem),
            input_output_aliases={len(units) + 1: 0, len(units) + 2: 1},
            compiler_params=params,
            cost_estimate=light,
        )(band, *blocks, unit, tall)

    mine, other = 0, 1
    sent, band = lax.optimization_barrier((diagonal, band))
    unit, tall = more(
        ((ABOVE, mine), (BELOW, mine), (PARTNER, mine), (DIAGONAL, other)),
        (above, below, partner, swap(sent)), unit, tall,
    )
    units = ((ABOVE, other), (BELOW, other), (PARTNER, other))
    _, _, out = pl.pallas_call(
        functools.partial(stack_kernel, scale, units),
        out_shape=(unit_shape, tall_shape, out_shape),
        in_specs=[smem, smem] + [vmem] * (len(units) + 3),
        out_specs=(vmem, vmem, hbm),
        input_output_aliases={len(units) + 3: 0, len(units) + 4: 1},
        scratch_shapes=[
            pltpu.VMEM((2, (FINE + 1) * half_rows, halves * length), jnp.bfloat16),
            pltpu.VMEM((cap, lags, half_rows, rows), jnp.float32),
            pltpu.SemaphoreType.DMA((2 * cap,)),
        ],
        compiler_params=params,
        cost_estimate=heavy,
    )(pairs, count, band, swap(above), swap(below), swap(partner), unit, tall)
    return jnp.transpose(out, (0, 2, 1, 3))


def solution(mesh):
    return jax.shard_map(
        body,
        mesh=mesh,
        in_specs=(
            P(("groups", "chan"), "tm", None),
            P(),
            P(("groups", "chan"), None),
            P(("groups", "chan")),
        ),
        out_specs=P(("groups", "chan"), "tm", None, None),
        check_vma=False,
    )
```

```python
import functools

import jax
import jax.numpy as jnp
from jax import lax
from jax.experimental import pallas as pl
from jax.experimental.pallas import tpu as pltpu
from jax.sharding import PartitionSpec as P

LAG = 32
REACH = 2
NEAR = 2 * REACH + 1
FINE = 8
COARSE = LAG // FINE
CHUNK = 4
COPIES = COARSE * (FINE // CHUNK) + 1
LANES = 128
TILE = 256
MARGIN = 32
OWN, PARTNER, BELOW, ABOVE, DIAGONAL = range(NEAR)


def passed(block, axis, target):
    size = lax.axis_size(axis)
    route = [(i, target(i)) for i in range(size) if 0 <= target(i) < size]
    return lax.ppermute(block, axis, route)


def partner_of(i):
    return i + 1 if i % 2 == 0 else i - 1


def diagonal_of(i):
    return i - 1 if i % 2 == 0 else i + 1


def place_of(block, owner):
    offset = block - owner
    side = jnp.where(offset == 1 - 2 * lax.rem(owner, 2), PARTNER, DIAGONAL)
    away = jnp.where(offset == -REACH, BELOW, jnp.where(offset == REACH, ABOVE, side))
    return jnp.where(offset == 0, OWN, away)


def shifted(rows, amount):
    if amount == 0:
        return rows
    length = rows.shape[-1]
    moved = pltpu.roll(rows, amount % length, 1)
    edge = slice(0, LANES) if amount > 0 else slice(length - LANES, length)
    lane = lax.broadcasted_iota(jnp.int32, (rows.shape[0], LANES), 1)
    keep = lane >= amount if amount > 0 else lane < LANES + amount
    cut = jnp.where(keep, moved[:, edge], jnp.zeros((), rows.dtype))
    if amount > 0:
        return jnp.concatenate([cut, moved[:, LANES:]], axis=1)
    return jnp.concatenate([moved[:, : length - LANES], cut], axis=1)


def make_band(taps_ref, band_ref):
    taps = taps_ref[...]
    wide = jnp.concatenate([taps, jnp.zeros((1, TILE - taps.shape[1]), jnp.float32)], axis=1)
    band = pltpu.roll(jnp.broadcast_to(wide, (TILE, TILE)), 0, 1, stride=1, stride_axis=0)
    row = lax.broadcasted_iota(jnp.int32, (TILE, TILE), 0)
    column = lax.broadcasted_iota(jnp.int32, (TILE, TILE), 1)
    band_ref[0] = jnp.where(column >= row, band, 0.0).astype(jnp.bfloat16)
    band_ref[1] = jnp.where(column < row, band, 0.0).astype(jnp.bfloat16)


def normalise(source_ref, band_ref, unit_ref, tall_ref, place, window):
    rows, length = unit_ref.shape[1], source_ref.shape[-1]
    tiles = length // TILE
    stacked = jnp.concatenate(
        [source_ref[:rows, tile * TILE : (tile + 1) * TILE] for tile in range(tiles)], axis=0
    )
    here = jnp.dot(stacked, band_ref[0], preferred_element_type=jnp.float32)
    after = jnp.dot(stacked[:-rows], band_ref[1], preferred_element_type=jnp.float32)
    pieces = [here[:rows]] + [
        here[tile * rows : (tile + 1) * rows] + after[(tile - 1) * rows : tile * rows]
        for tile in range(1, tiles)
    ]
    filtered = jnp.concatenate(pieces, axis=1)
    meansq = jnp.mean(filtered * filtered, axis=-1, keepdims=True)
    unit = filtered * lax.rsqrt(meansq + 1e-06)
    unit_ref[place, :, window * length : (window + 1) * length] = unit.astype(jnp.bfloat16)
    tall = unit.T
    gap = jnp.zeros((FINE, rows), jnp.float32)
    edge = jnp.zeros((MARGIN, rows), jnp.bfloat16)
    inner = MARGIN - 2 * FINE
    for phase in range(2):
        tall_ref[place, window, phase, :MARGIN] = edge
        tall_ref[place, window, phase, length + MARGIN :] = edge
    tall_ref[place, window, 0, MARGIN : MARGIN + length] = tall.astype(jnp.bfloat16)
    tall_ref[place, window, 1, inner : inner + length + 2 * FINE] = jnp.concatenate(
        [gap, tall, gap], axis=0
    ).astype(jnp.bfloat16)


def prepare(source, sign, unit_ref, left_ref, half_rows):
    length = unit_ref.shape[2] // 2
    first_row = pl.multiple_of(lax.axis_index("tm") * half_rows, half_rows)
    for window in range(2):
        span = slice(window * length, (window + 1) * length)
        rows = unit_ref[source, pl.ds(first_row, half_rows), span]
        for place in range(FINE + 1 if sign > 0 else FINE):
            step = place if sign > 0 else place - FINE
            left_ref[place * half_rows : (place + 1) * half_rows, span] = shifted(rows, step)


def coarse_rows(tall_ref, partner, window, amount):
    length = tall_ref.shape[3] - 2 * MARGIN
    phase = amount // FINE % 2
    first = MARGIN + amount - FINE * phase
    return tall_ref[partner, window, phase, first : first + length]


def coarse_columns(tall_ref, partner, amounts):
    return jnp.concatenate(
        [
            jnp.concatenate(
                [coarse_rows(tall_ref, partner, window, amount) for amount in amounts], axis=1
            )
            for window in range(2)
        ],
        axis=0,
    )


def correlate(slot, sign, factor, partner, left_ref, tall_ref, stage_ref, out_ref, sems):
    half_rows, channels = stage_ref.shape[1:]
    amounts = [sign * FINE * place for place in range(COARSE)]
    first = 0 if sign > 0 else -FINE
    copies = []

    def product(steps, amounts):
        low = steps[0] - first
        result = jnp.dot(
            left_ref[low * half_rows : (low + len(steps)) * half_rows, :],
            coarse_columns(tall_ref, partner, amounts), preferred_element_type=jnp.float32,
        )
        for column, amount in enumerate(amounts):
            for row, step in enumerate(steps):
                stage_ref[LAG + amount + step] = factor * result[
                    row * half_rows : (row + 1) * half_rows,
                    column * channels : (column + 1) * channels,
                ]
            span = pl.ds(LAG + amount + steps[0], len(steps))
            copy = pltpu.make_async_copy(
                stage_ref.at[span], out_ref.at[slot, span], sems.at[len(copies)]
            )
            copy.start()
            copies.append(copy)

    if sign > 0:
        product([FINE], amounts[-1:])
    for part in range(0, FINE, CHUNK):
        product(range(first + part, first + part + CHUNK), amounts)
    return copies


def early_kernel(pairs_ref, count_ref, taps_ref, *refs):
    blocks, (band_ref, unit_ref, tall_ref) = refs[:3], refs[3:]
    make_band(taps_ref, band_ref)
    for block, (place, window) in zip(blocks, ((OWN, 0), (OWN, 1), (DIAGONAL, 0))):
        normalise(block, band_ref, unit_ref, tall_ref, place, window)


def filter_kernel(units, band_ref, *refs):
    blocks, (unit_ref, tall_ref) = refs[: len(units)], refs[len(units) + 2 :]
    for block, (place, window) in zip(blocks, units):
        normalise(block, band_ref, unit_ref, tall_ref, place, window)


def stack_kernel(scale, units, pairs_ref, count_ref, band_ref, *refs):
    blocks, refs = refs[: len(units)], refs[len(units) + 2 :]
    unit_ref, tall_ref, out_ref, left_ref, stage_ref, sems = refs
    for block, (place, window) in zip(blocks, units):
        normalise(block, band_ref, unit_ref, tall_ref, place, window)
    slots = out_ref.shape[0]
    steps = [(slot, sign) for slot in range(slots) for sign in (1, -1)]
    owner = lax.axis_index("chan")

    def ready(number):
        if number < len(steps):
            slot, sign = steps[number]
            source = place_of(pairs_ref[0, slot], owner)
            prepare(source, sign, unit_ref, left_ref.at[number % 2], stage_ref.shape[2])

    copies = []
    ready(0)
    for number, (slot, sign) in enumerate(steps):
        ready(number + 1)
        factor = jnp.where(slot < count_ref[0], scale, 0.0)
        partner = place_of(pairs_ref[1, slot], owner)
        copies += (
            correlate(
                slot, sign, factor, partner, left_ref.at[number % 2], tall_ref,
                stage_ref.at[slot], out_ref, sems.at[number],
            )
        )
    for copy in copies:
        copy.wait()


def body(traces, fir_taps, pair_blocks, pair_count):
    rows, windows, length = traces.shape
    own = traces.reshape(rows, length)
    halves = lax.axis_size("tm")
    cap = pair_blocks.shape[0]
    lags = 2 * LAG + 1
    half_rows = rows // halves
    scale = float(windows * halves * length) ** (-0.5)

    swap = lambda array: passed(array, "tm", lambda i: 1 - i)
    partner = passed(own, "chan", partner_of)
    below = passed(own, "chan", lambda i: i + REACH)
    above = passed(own, "chan", lambda i: i - REACH)
    diagonal = passed(own, "chan", diagonal_of)
    pairs, count = pair_blocks.T, pair_count
    taps = fir_taps.astype(jnp.float32)[None, :]

    smem = pl.BlockSpec(memory_space=pltpu.SMEM)
    vmem = pl.BlockSpec(memory_space=pltpu.VMEM)
    hbm = pl.BlockSpec(memory_space=pl.ANY)
    params = pltpu.CompilerParams(vmem_limit_bytes=32 * 1024 * 1024)
    band_shape = jax.ShapeDtypeStruct((2, TILE, TILE), jnp.bfloat16)
    unit_shape = jax.ShapeDtypeStruct((NEAR, rows, halves * length), jnp.bfloat16)
    tall_shape = jax.ShapeDtypeStruct(
        (NEAR, halves, 2, length + 2 * MARGIN, rows), jnp.bfloat16
    )
    out_shape = jax.ShapeDtypeStruct((cap, lags, half_rows, rows), jnp.float32)
    light = pl.CostEstimate(flops=1, bytes_accessed=1, transcendentals=0)
    heavy = pl.CostEstimate(
        flops=2 * cap * lags * half_rows * rows * halves * length,
        bytes_accessed=cap * lags * half_rows * rows * 4,
        transcendentals=0,
    )

    band, unit, tall = pl.pallas_call(
        early_kernel,
        out_shape=(band_shape, unit_shape, tall_shape),
        in_specs=[smem, smem] + [vmem] * 4,
        out_specs=(vmem, vmem, vmem),
        compiler_params=params,
        cost_estimate=light,
    )(pairs, count, taps, own, swap(own), diagonal)

    def more(units, blocks, unit, tall):
        return pl.pallas_call(
            functools.partial(filter_kernel, units),
            out_shape=(unit_shape, tall_shape),
            in_specs=[vmem] * (len(units) + 3),
            out_specs=(vmem, vmem),
            input_output_aliases={len(units) + 1: 0, len(units) + 2: 1},
            compiler_params=params,
            cost_estimate=light,
        )(band, *blocks, unit, tall)

    mine, other = 0, 1
    sent, band = lax.optimization_barrier((diagonal, band))
    unit, tall = more(
        ((BELOW, mine), (ABOVE, mine), (PARTNER, mine), (DIAGONAL, other)),
        (below, above, partner, swap(sent)), unit, tall,
    )
    units = ((BELOW, other), (ABOVE, other), (PARTNER, other))
    _, _, out = pl.pallas_call(
        functools.partial(stack_kernel, scale, units),
        out_shape=(unit_shape, tall_shape, out_shape),
        in_specs=[smem, smem] + [vmem] * (len(units) + 3),
        out_specs=(vmem, vmem, hbm),
        input_output_aliases={len(units) + 3: 0, len(units) + 4: 1},
        scratch_shapes=[
            pltpu.VMEM((2, (FINE + 1) * half_rows, halves * length), jnp.bfloat16),
            pltpu.VMEM((cap, lags, half_rows, rows), jnp.float32),
            pltpu.SemaphoreType.DMA((2 * cap, COPIES)),
        ],
        compiler_params=params,
        cost_estimate=heavy,
    )(pairs, count, band, swap(below), swap(above), swap(partner), unit, tall)
    return jnp.transpose(out, (0, 2, 1, 3))


def solution(mesh):
    return jax.shard_map(
        body,
        mesh=mesh,
        in_specs=(
            P(("groups", "chan"), "tm", None),
            P(),
            P(("groups", "chan"), None),
            P(("groups", "chan")),
        ),
        out_specs=P(("groups", "chan"), "tm", None, None),
        check_vma=False,
    )
```

```python
import functools

import jax
import jax.numpy as jnp
from jax import lax
from jax.experimental import pallas as pl
from jax.experimental.pallas import tpu as pltpu
from jax.sharding import PartitionSpec as P

LAG = 32
REACH = 2
NEAR = 2 * REACH + 1
FINE = 8
COARSE = LAG // FINE
CHUNK = 8
COPIES = COARSE * (FINE // CHUNK) + 1
LANES = 128
TILE = 256
MARGIN = 32
OWN, PARTNER, BELOW, ABOVE, DIAGONAL = range(NEAR)


def passed(block, axis, target):
    size = lax.axis_size(axis)
    route = [(i, target(i)) for i in range(size) if 0 <= target(i) < size]
    return lax.ppermute(block, axis, route)


def partner_of(i):
    return i + 1 if i % 2 == 0 else i - 1


def diagonal_of(i):
    return i - 1 if i % 2 == 0 else i + 1


def place_of(block, owner):
    offset = block - owner
    side = jnp.where(offset == 1 - 2 * lax.rem(owner, 2), PARTNER, DIAGONAL)
    away = jnp.where(offset == -REACH, BELOW, jnp.where(offset == REACH, ABOVE, side))
    return jnp.where(offset == 0, OWN, away)


def shifted(rows, amount):
    if amount == 0:
        return rows
    length = rows.shape[-1]
    moved = pltpu.roll(rows, amount % length, 1)
    edge = slice(0, LANES) if amount > 0 else slice(length - LANES, length)
    lane = lax.broadcasted_iota(jnp.int32, (rows.shape[0], LANES), 1)
    keep = lane >= amount if amount > 0 else lane < LANES + amount
    cut = jnp.where(keep, moved[:, edge], jnp.zeros((), rows.dtype))
    if amount > 0:
        return jnp.concatenate([cut, moved[:, LANES:]], axis=1)
    return jnp.concatenate([moved[:, : length - LANES], cut], axis=1)


def make_band(taps_ref, band_ref):
    taps = taps_ref[...]
    wide = jnp.concatenate([taps, jnp.zeros((1, TILE - taps.shape[1]), jnp.float32)], axis=1)
    band = pltpu.roll(jnp.broadcast_to(wide, (TILE, TILE)), 0, 1, stride=1, stride_axis=0)
    row = lax.broadcasted_iota(jnp.int32, (TILE, TILE), 0)
    column = lax.broadcasted_iota(jnp.int32, (TILE, TILE), 1)
    band_ref[0] = jnp.where(column >= row, band, 0.0).astype(jnp.bfloat16)
    band_ref[1] = jnp.where(column < row, band, 0.0).astype(jnp.bfloat16)


def normalise(source_ref, band_ref, unit_ref, tall_ref, place, window):
    rows, length = unit_ref.shape[1], source_ref.shape[-1]
    tiles = length // TILE
    stacked = jnp.concatenate(
        [source_ref[:rows, tile * TILE : (tile + 1) * TILE] for tile in range(tiles)], axis=0
    )
    here = jnp.dot(stacked, band_ref[0], preferred_element_type=jnp.float32)
    after = jnp.dot(stacked[:-rows], band_ref[1], preferred_element_type=jnp.float32)
    pieces = [here[:rows]] + [
        here[tile * rows : (tile + 1) * rows] + after[(tile - 1) * rows : tile * rows]
        for tile in range(1, tiles)
    ]
    filtered = jnp.concatenate(pieces, axis=1)
    meansq = jnp.mean(filtered * filtered, axis=-1, keepdims=True)
    unit = filtered * lax.rsqrt(meansq + 1e-06)
    unit_ref[place, :, window * length : (window + 1) * length] = unit.astype(jnp.bfloat16)
    tall = unit.T
    gap = jnp.zeros((FINE, rows), jnp.float32)
    edge = jnp.zeros((MARGIN, rows), jnp.bfloat16)
    inner = MARGIN - 2 * FINE
    for phase in range(2):
        tall_ref[place, window, phase, :MARGIN] = edge
        tall_ref[place, window, phase, length + MARGIN :] = edge
    tall_ref[place, window, 0, MARGIN : MARGIN + length] = tall.astype(jnp.bfloat16)
    tall_ref[place, window, 1, inner : inner + length + 2 * FINE] = jnp.concatenate(
        [gap, tall, gap], axis=0
    ).astype(jnp.bfloat16)


def prepare(source, sign, unit_ref, left_ref, half_rows):
    length = unit_ref.shape[2] // 2
    first_row = pl.multiple_of(lax.axis_index("tm") * half_rows, half_rows)
    for window in range(2):
        span = slice(window * length, (window + 1) * length)
        rows = unit_ref[source, pl.ds(first_row, half_rows), span]
        for place in range(FINE + 1 if sign > 0 else FINE):
            step = place if sign > 0 else place - FINE
            left_ref[place * half_rows : (place + 1) * half_rows, span] = shifted(rows, step)


def coarse_rows(tall_ref, partner, window, amount):
    length = tall_ref.shape[3] - 2 * MARGIN
    phase = amount // FINE % 2
    first = MARGIN + amount - FINE * phase
    return tall_ref[partner, window, phase, first : first + length]


def coarse_columns(tall_ref, partner, amounts):
    return jnp.concatenate(
        [
            jnp.concatenate(
                [coarse_rows(tall_ref, partner, window, amount) for amount in amounts], axis=1
            )
            for window in range(2)
        ],
        axis=0,
    )


def correlate(slot, sign, factor, partner, left_ref, tall_ref, stage_ref, out_ref, sems):
    half_rows, channels = stage_ref.shape[1:]
    amounts = [sign * FINE * place for place in range(COARSE)]
    first = 0 if sign > 0 else -FINE
    copies = []

    def product(steps, amounts):
        low = steps[0] - first
        result = jnp.dot(
            left_ref[low * half_rows : (low + len(steps)) * half_rows, :],
            coarse_columns(tall_ref, partner, amounts), preferred_element_type=jnp.float32,
        )
        for column, amount in enumerate(amounts):
            for row, step in enumerate(steps):
                stage_ref[LAG + amount + step] = factor * result[
                    row * half_rows : (row + 1) * half_rows,
                    column * channels : (column + 1) * channels,
                ]
            span = pl.ds(LAG + amount + steps[0], len(steps))
            copy = pltpu.make_async_copy(
                stage_ref.at[span], out_ref.at[slot, span], sems.at[len(copies)]
            )
            copy.start()
            copies.append(copy)

    if sign > 0:
        product([FINE], amounts[-1:])
    for part in range(0, FINE, CHUNK):
        product(range(first + part, first + part + CHUNK), amounts)
    return copies


def early_kernel(pairs_ref, count_ref, taps_ref, *refs):
    blocks, (band_ref, unit_ref, tall_ref) = refs[:3], refs[3:]
    make_band(taps_ref, band_ref)
    for block, (place, window) in zip(blocks, ((OWN, 0), (OWN, 1), (DIAGONAL, 0))):
        normalise(block, band_ref, unit_ref, tall_ref, place, window)


def filter_kernel(units, band_ref, *refs):
    blocks, (unit_ref, tall_ref) = refs[: len(units)], refs[len(units) + 2 :]
    for block, (place, window) in zip(blocks, units):
        normalise(block, band_ref, unit_ref, tall_ref, place, window)


def stack_kernel(scale, units, pairs_ref, count_ref, band_ref, *refs):
    blocks, refs = refs[: len(units)], refs[len(units) + 2 :]
    unit_ref, tall_ref, out_ref, left_ref, stage_ref, sems = refs
    for block, (place, window) in zip(blocks, units):
        normalise(block, band_ref, unit_ref, tall_ref, place, window)
    slots = out_ref.shape[0]
    steps = [(slot, sign) for slot in range(slots) for sign in (1, -1)]
    owner = lax.axis_index("chan")

    def ready(number):
        if number < len(steps):
            slot, sign = steps[number]
            source = place_of(pairs_ref[0, slot], owner)
            prepare(source, sign, unit_ref, left_ref.at[number % 2], stage_ref.shape[2])

    copies = []
    ready(0)
    for number, (slot, sign) in enumerate(steps):
        ready(number + 1)
        factor = jnp.where(slot < count_ref[0], scale, 0.0)
        partner = place_of(pairs_ref[1, slot], owner)
        copies += (
            correlate(
                slot, sign, factor, partner, left_ref.at[number % 2], tall_ref,
                stage_ref.at[slot], out_ref, sems.at[number],
            )
        )
    for copy in copies:
        copy.wait()


def body(traces, fir_taps, pair_blocks, pair_count):
    rows, windows, length = traces.shape
    own = traces.reshape(rows, length)
    halves = lax.axis_size("tm")
    cap = pair_blocks.shape[0]
    lags = 2 * LAG + 1
    half_rows = rows // halves
    scale = float(windows * halves * length) ** (-0.5)

    swap = lambda array: passed(array, "tm", lambda i: 1 - i)
    partner = passed(own, "chan", partner_of)
    below = passed(own, "chan", lambda i: i + REACH)
    above = passed(own, "chan", lambda i: i - REACH)
    diagonal = passed(own, "chan", diagonal_of)
    pairs, count = pair_blocks.T, pair_count
    taps = fir_taps.astype(jnp.float32)[None, :]

    smem = pl.BlockSpec(memory_space=pltpu.SMEM)
    vmem = pl.BlockSpec(memory_space=pltpu.VMEM)
    hbm = pl.BlockSpec(memory_space=pl.ANY)
    params = pltpu.CompilerParams(vmem_limit_bytes=32 * 1024 * 1024)
    band_shape = jax.ShapeDtypeStruct((2, TILE, TILE), jnp.bfloat16)
    unit_shape = jax.ShapeDtypeStruct((NEAR, rows, halves * length), jnp.bfloat16)
    tall_shape = jax.ShapeDtypeStruct(
        (NEAR, halves, 2, length + 2 * MARGIN, rows), jnp.bfloat16
    )
    out_shape = jax.ShapeDtypeStruct((cap, lags, half_rows, rows), jnp.float32)
    light = pl.CostEstimate(flops=1, bytes_accessed=1, transcendentals=0)
    heavy = pl.CostEstimate(
        flops=2 * cap * lags * half_rows * rows * halves * length,
        bytes_accessed=cap * lags * half_rows * rows * 4,
        transcendentals=0,
    )

    band, unit, tall = pl.pallas_call(
        early_kernel,
        out_shape=(band_shape, unit_shape, tall_shape),
        in_specs=[smem, smem] + [vmem] * 4,
        out_specs=(vmem, vmem, vmem),
        compiler_params=params,
        cost_estimate=light,
    )(pairs, count, taps, own, swap(own), diagonal)

    def more(units, blocks, unit, tall):
        return pl.pallas_call(
            functools.partial(filter_kernel, units),
            out_shape=(unit_shape, tall_shape),
            in_specs=[vmem] * (len(units) + 3),
            out_specs=(vmem, vmem),
            input_output_aliases={len(units) + 1: 0, len(units) + 2: 1},
            compiler_params=params,
            cost_estimate=light,
        )(band, *blocks, unit, tall)

    mine, other = 0, 1
    sent, band = lax.optimization_barrier((diagonal, band))
    unit, tall = more(
        ((BELOW, mine), (PARTNER, mine), (ABOVE, mine), (DIAGONAL, other)),
        (below, partner, above, swap(sent)), unit, tall,
    )
    units = ((BELOW, other), (PARTNER, other), (ABOVE, other))
    _, _, out = pl.pallas_call(
        functools.partial(stack_kernel, scale, units),
        out_shape=(unit_shape, tall_shape, out_shape),
        in_specs=[smem, smem] + [vmem] * (len(units) + 3),
        out_specs=(vmem, vmem, hbm),
        input_output_aliases={len(units) + 3: 0, len(units) + 4: 1},
        scratch_shapes=[
            pltpu.VMEM((2, (FINE + 1) * half_rows, halves * length), jnp.bfloat16),
            pltpu.VMEM((cap, lags, half_rows, rows), jnp.float32),
            pltpu.SemaphoreType.DMA((2 * cap, COPIES)),
        ],
        compiler_params=params,
        cost_estimate=heavy,
    )(pairs, count, band, swap(below), swap(partner), swap(above), unit, tall)
    return jnp.transpose(out, (0, 2, 1, 3))


def solution(mesh):
    return jax.shard_map(
        body,
        mesh=mesh,
        in_specs=(
            P(("groups", "chan"), "tm", None),
            P(),
            P(("groups", "chan"), None),
            P(("groups", "chan")),
        ),
        out_specs=P(("groups", "chan"), "tm", None, None),
        check_vma=False,
    )
```

```python
import functools

import jax
import jax.numpy as jnp
from jax import lax
from jax.experimental import pallas as pl
from jax.experimental.pallas import tpu as pltpu
from jax.sharding import PartitionSpec as P

LAG = 32
REACH = 2
NEAR = 2 * REACH + 1
FINE = 8
COARSE = LAG // FINE
LANES = 128
TILE = 256
MARGIN = 32
OWN, PARTNER, BELOW, ABOVE, DIAGONAL = range(NEAR)


def passed(block, axis, target):
    size = lax.axis_size(axis)
    route = [(i, target(i)) for i in range(size) if 0 <= target(i) < size]
    return lax.ppermute(block, axis, route)


def partner_of(i):
    return i + 1 if i % 2 == 0 else i - 1


def diagonal_of(i):
    return i - 1 if i % 2 == 0 else i + 1


def place_of(block, owner):
    offset = block - owner
    side = jnp.where(offset == 1 - 2 * lax.rem(owner, 2), PARTNER, DIAGONAL)
    away = jnp.where(offset == -REACH, BELOW, jnp.where(offset == REACH, ABOVE, side))
    return jnp.where(offset == 0, OWN, away)


def shifted(rows, amount):
    if amount == 0:
        return rows
    length = rows.shape[-1]
    moved = pltpu.roll(rows, amount % length, 1)
    edge = slice(0, LANES) if amount > 0 else slice(length - LANES, length)
    lane = lax.broadcasted_iota(jnp.int32, (rows.shape[0], LANES), 1)
    keep = lane >= amount if amount > 0 else lane < LANES + amount
    cut = jnp.where(keep, moved[:, edge], jnp.zeros((), rows.dtype))
    if amount > 0:
        return jnp.concatenate([cut, moved[:, LANES:]], axis=1)
    return jnp.concatenate([moved[:, : length - LANES], cut], axis=1)


def make_band(taps_ref, band_ref):
    taps = taps_ref[...]
    wide = jnp.concatenate([taps, jnp.zeros((1, TILE - taps.shape[1]), jnp.float32)], axis=1)
    band = pltpu.roll(jnp.broadcast_to(wide, (TILE, TILE)), 0, 1, stride=1, stride_axis=0)
    row = lax.broadcasted_iota(jnp.int32, (TILE, TILE), 0)
    column = lax.broadcasted_iota(jnp.int32, (TILE, TILE), 1)
    band_ref[0] = jnp.where(column >= row, band, 0.0).astype(jnp.bfloat16)
    band_ref[1] = jnp.where(column < row, band, 0.0).astype(jnp.bfloat16)


def normalise(source_ref, band_ref, unit_ref, tall_ref, place, window):
    rows, length = unit_ref.shape[1], source_ref.shape[-1]
    tiles = length // TILE
    stacked = jnp.concatenate(
        [source_ref[:rows, tile * TILE : (tile + 1) * TILE] for tile in range(tiles)], axis=0
    )
    here = jnp.dot(stacked, band_ref[0], preferred_element_type=jnp.float32)
    after = jnp.dot(stacked[:-rows], band_ref[1], preferred_element_type=jnp.float32)
    pieces = [here[:rows]] + [
        here[tile * rows : (tile + 1) * rows] + after[(tile - 1) * rows : tile * rows]
        for tile in range(1, tiles)
    ]
    filtered = jnp.concatenate(pieces, axis=1)
    meansq = jnp.mean(filtered * filtered, axis=-1, keepdims=True)
    unit = filtered * lax.rsqrt(meansq + 1e-06)
    unit_ref[place, :, window * length : (window + 1) * length] = unit.astype(jnp.bfloat16)
    tall = unit.T
    gap = jnp.zeros((FINE, rows), jnp.float32)
    edge = jnp.zeros((MARGIN, rows), jnp.bfloat16)
    inner = MARGIN - 2 * FINE
    for phase in range(2):
        tall_ref[place, window, phase, :MARGIN] = edge
        tall_ref[place, window, phase, length + MARGIN :] = edge
    tall_ref[place, window, 0, MARGIN : MARGIN + length] = tall.astype(jnp.bfloat16)
    tall_ref[place, window, 1, inner : inner + length + 2 * FINE] = jnp.concatenate(
        [gap, tall, gap], axis=0
    ).astype(jnp.bfloat16)


def own_rows(source, unit_ref, half_rows, span):
    first = pl.multiple_of(lax.axis_index("tm") * half_rows, half_rows)
    return unit_ref[source, pl.ds(first, half_rows), span]


def fine_steps(sign):
    return range(1, FINE + 1) if sign > 0 else range(-FINE, 0)


def prepare(source, sign, unit_ref, left_ref, half_rows):
    length = unit_ref.shape[2] // 2
    for window in range(2):
        span = slice(window * length, (window + 1) * length)
        rows = own_rows(source, unit_ref, half_rows, span)
        for row, step in enumerate(fine_steps(sign)):
            left_ref[row * half_rows : (row + 1) * half_rows, span] = shifted(rows, step)


def coarse_rows(tall_ref, partner, window, amount):
    length = tall_ref.shape[3] - 2 * MARGIN
    phase = amount // FINE % 2
    first = MARGIN + amount - FINE * phase
    return tall_ref[partner, window, phase, first : first + length]


def coarse_columns(tall_ref, partner, amounts):
    return jnp.concatenate(
        [
            jnp.concatenate(
                [coarse_rows(tall_ref, partner, window, amount) for amount in amounts], axis=1
            )
            for window in range(2)
        ],
        axis=0,
    )


def correlate(sign, factor, partner, left_ref, tall_ref, stage_ref):
    half_rows, channels = stage_ref.shape[1:]
    amounts = [sign * FINE * place for place in range(COARSE)]
    result = jnp.dot(
        left_ref[...], coarse_columns(tall_ref, partner, amounts),
        preferred_element_type=jnp.float32,
    )
    for column, amount in enumerate(amounts):
        for row, step in enumerate(fine_steps(sign)):
            stage_ref[LAG + amount + step] = factor * result[
                row * half_rows : (row + 1) * half_rows,
                column * channels : (column + 1) * channels,
            ]


def early_kernel(pairs_ref, count_ref, taps_ref, *refs):
    blocks, (band_ref, unit_ref, tall_ref) = refs[:3], refs[3:]
    make_band(taps_ref, band_ref)
    for block, (place, window) in zip(blocks, ((OWN, 0), (OWN, 1), (DIAGONAL, 0))):
        normalise(block, band_ref, unit_ref, tall_ref, place, window)


def filter_kernel(units, band_ref, *refs):
    blocks, (unit_ref, tall_ref) = refs[: len(units)], refs[len(units) + 2 :]
    for block, (place, window) in zip(blocks, units):
        normalise(block, band_ref, unit_ref, tall_ref, place, window)


def stack_kernel(scale, units, pairs_ref, count_ref, band_ref, *refs):
    blocks, refs = refs[: len(units)], refs[len(units) + 2 :]
    unit_ref, tall_ref, out_ref, left_ref, stage_ref, sems = refs
    for block, (place, window) in zip(blocks, units):
        normalise(block, band_ref, unit_ref, tall_ref, place, window)
    slots, lags, half_rows, _ = out_ref.shape
    owner = lax.axis_index("chan")

    def ready(slot):
        if slot < slots:
            source = place_of(pairs_ref[0, slot], owner)
            for side, sign in enumerate((1, -1)):
                prepare(source, sign, unit_ref, left_ref.at[slot % 2, side], half_rows)

    copies = []

    def send(slot, first, count):
        span = pl.ds(first, count)
        copy = pltpu.make_async_copy(
            stage_ref.at[slot, span], out_ref.at[slot, span], sems.at[len(copies)]
        )
        copy.start()
        copies.append(copy)

    ready(0)
    for slot in range(slots):
        ready(slot + 1)
        factor = jnp.where(slot < count_ref[0], scale, 0.0)
        source = place_of(pairs_ref[0, slot], owner)
        partner = place_of(pairs_ref[1, slot], owner)
        for side, sign in enumerate((1, -1)):
            correlate(
                sign, factor, partner, left_ref.at[slot % 2, side], tall_ref, stage_ref.at[slot]
            )
            if sign > 0:
                stage_ref[slot, LAG] = factor * jnp.dot(
                    own_rows(source, unit_ref, half_rows, slice(None)),
                    coarse_columns(tall_ref, partner, [0]), preferred_element_type=jnp.float32,
                )
                if slot == slots - 1:
                    send(slot, LAG, lags - LAG)
        if slot == slots - 1:
            send(slot, 0, LAG)
        else:
            send(slot, 0, lags)
    for copy in copies:
        copy.wait()


def body(traces, fir_taps, pair_blocks, pair_count):
    rows, windows, length = traces.shape
    own = traces.reshape(rows, length)
    halves = lax.axis_size("tm")
    cap = pair_blocks.shape[0]
    lags = 2 * LAG + 1
    half_rows = rows // halves
    scale = float(windows * halves * length) ** (-0.5)

    swap = lambda array: passed(array, "tm", lambda i: 1 - i)
    partner = passed(own, "chan", partner_of)
    below = passed(own, "chan", lambda i: i + REACH)
    above = passed(own, "chan", lambda i: i - REACH)
    diagonal = passed(own, "chan", diagonal_of)
    pairs, count = pair_blocks.T, pair_count
    taps = fir_taps.astype(jnp.float32)[None, :]

    smem = pl.BlockSpec(memory_space=pltpu.SMEM)
    vmem = pl.BlockSpec(memory_space=pltpu.VMEM)
    hbm = pl.BlockSpec(memory_space=pl.ANY)
    params = pltpu.CompilerParams(vmem_limit_bytes=32 * 1024 * 1024)
    band_shape = jax.ShapeDtypeStruct((2, TILE, TILE), jnp.bfloat16)
    unit_shape = jax.ShapeDtypeStruct((NEAR, rows, halves * length), jnp.bfloat16)
    tall_shape = jax.ShapeDtypeStruct(
        (NEAR, halves, 2, length + 2 * MARGIN, rows), jnp.bfloat16
    )
    out_shape = jax.ShapeDtypeStruct((cap, lags, half_rows, rows), jnp.float32)
    light = pl.CostEstimate(flops=1, bytes_accessed=1, transcendentals=0)
    heavy = pl.CostEstimate(
        flops=2 * cap * lags * half_rows * rows * halves * length,
        bytes_accessed=cap * lags * half_rows * rows * 4,
        transcendentals=0,
    )

    band, unit, tall = pl.pallas_call(
        early_kernel,
        out_shape=(band_shape, unit_shape, tall_shape),
        in_specs=[smem, smem] + [vmem] * 4,
        out_specs=(vmem, vmem, vmem),
        compiler_params=params,
        cost_estimate=light,
    )(pairs, count, taps, own, swap(own), diagonal)

    def more(units, blocks, unit, tall):
        return pl.pallas_call(
            functools.partial(filter_kernel, units),
            out_shape=(unit_shape, tall_shape),
            in_specs=[vmem] * (len(units) + 3),
            out_specs=(vmem, vmem),
            input_output_aliases={len(units) + 1: 0, len(units) + 2: 1},
            compiler_params=params,
            cost_estimate=light,
        )(band, *blocks, unit, tall)

    mine, other = 0, 1
    sent, band = lax.optimization_barrier((diagonal, band))
    unit, tall = more(
        ((BELOW, mine), (ABOVE, mine), (PARTNER, mine), (DIAGONAL, other)),
        (below, above, partner, swap(sent)), unit, tall,
    )
    units = ((BELOW, other), (ABOVE, other), (PARTNER, other))
    _, _, out = pl.pallas_call(
        functools.partial(stack_kernel, scale, units),
        out_shape=(unit_shape, tall_shape, out_shape),
        in_specs=[smem, smem] + [vmem] * (len(units) + 3),
        out_specs=(vmem, vmem, hbm),
        input_output_aliases={len(units) + 3: 0, len(units) + 4: 1},
        scratch_shapes=[
            pltpu.VMEM((2, 2, FINE * half_rows, halves * length), jnp.bfloat16),
            pltpu.VMEM((cap, lags, half_rows, rows), jnp.float32),
            pltpu.SemaphoreType.DMA((cap + 1,)),
        ],
        compiler_params=params,
        cost_estimate=heavy,
    )(pairs, count, band, swap(below), swap(above), swap(partner), unit, tall)
    return jnp.transpose(out, (0, 2, 1, 3))


def solution(mesh):
    return jax.shard_map(
        body,
        mesh=mesh,
        in_specs=(
            P(("groups", "chan"), "tm", None),
            P(),
            P(("groups", "chan"), None),
            P(("groups", "chan")),
        ),
        out_specs=P(("groups", "chan"), "tm", None, None),
        check_vma=False,
    )
```

```python
import functools

import jax
import jax.numpy as jnp
from jax import lax
from jax.experimental import pallas as pl
from jax.experimental.pallas import tpu as pltpu
from jax.sharding import PartitionSpec as P

LAG = 32
REACH = 2
NEAR = 2 * REACH + 1
FINE = 8
COARSE = LAG // FINE
TALL = 2
WIDE = 2
LANES = 128
TILE = 256
MARGIN = 32
OWN, PARTNER, BELOW, ABOVE, DIAGONAL = range(NEAR)


def passed(block, axis, target):
    size = lax.axis_size(axis)
    route = [(i, target(i)) for i in range(size) if 0 <= target(i) < size]
    return lax.ppermute(block, axis, route)


def partner_of(i):
    return i + 1 if i % 2 == 0 else i - 1


def diagonal_of(i):
    return i - 1 if i % 2 == 0 else i + 1


def place_of(block, owner):
    offset = block - owner
    side = jnp.where(offset == 1 - 2 * lax.rem(owner, 2), PARTNER, DIAGONAL)
    away = jnp.where(offset == -REACH, BELOW, jnp.where(offset == REACH, ABOVE, side))
    return jnp.where(offset == 0, OWN, away)


def shifted(rows, amount):
    if amount == 0:
        return rows
    length = rows.shape[-1]
    moved = pltpu.roll(rows, amount % length, 1)
    edge = slice(0, LANES) if amount > 0 else slice(length - LANES, length)
    lane = lax.broadcasted_iota(jnp.int32, (rows.shape[0], LANES), 1)
    keep = lane >= amount if amount > 0 else lane < LANES + amount
    cut = jnp.where(keep, moved[:, edge], jnp.zeros((), rows.dtype))
    if amount > 0:
        return jnp.concatenate([cut, moved[:, LANES:]], axis=1)
    return jnp.concatenate([moved[:, : length - LANES], cut], axis=1)


def make_band(taps_ref, band_ref):
    taps = taps_ref[...]
    wide = jnp.concatenate([taps, jnp.zeros((1, TILE - taps.shape[1]), jnp.float32)], axis=1)
    band = pltpu.roll(jnp.broadcast_to(wide, (TILE, TILE)), 0, 1, stride=1, stride_axis=0)
    row = lax.broadcasted_iota(jnp.int32, (TILE, TILE), 0)
    column = lax.broadcasted_iota(jnp.int32, (TILE, TILE), 1)
    band_ref[0] = jnp.where(column >= row, band, 0.0).astype(jnp.bfloat16)
    band_ref[1] = jnp.where(column < row, band, 0.0).astype(jnp.bfloat16)


def normalise(source_ref, band_ref, unit_ref, tall_ref, place, window):
    rows, length = unit_ref.shape[1], source_ref.shape[-1]
    tiles = length // TILE
    stacked = jnp.concatenate(
        [source_ref[:rows, tile * TILE : (tile + 1) * TILE] for tile in range(tiles)], axis=0
    )
    here = jnp.dot(stacked, band_ref[0], preferred_element_type=jnp.float32)
    after = jnp.dot(stacked[:-rows], band_ref[1], preferred_element_type=jnp.float32)
    pieces = [here[:rows]] + [
        here[tile * rows : (tile + 1) * rows] + after[(tile - 1) * rows : tile * rows]
        for tile in range(1, tiles)
    ]
    filtered = jnp.concatenate(pieces, axis=1)
    meansq = jnp.mean(filtered * filtered, axis=-1, keepdims=True)
    unit = filtered * lax.rsqrt(meansq + 1e-06)
    unit_ref[place, :, window * length : (window + 1) * length] = unit.astype(jnp.bfloat16)
    tall = unit.T
    gap = jnp.zeros((FINE, rows), jnp.float32)
    edge = jnp.zeros((MARGIN, rows), jnp.bfloat16)
    inner = MARGIN - 2 * FINE
    for phase in range(2):
        tall_ref[place, window, phase, :MARGIN] = edge
        tall_ref[place, window, phase, length + MARGIN :] = edge
    tall_ref[place, window, 0, MARGIN : MARGIN + length] = tall.astype(jnp.bfloat16)
    tall_ref[place, window, 1, inner : inner + length + 2 * FINE] = jnp.concatenate(
        [gap, tall, gap], axis=0
    ).astype(jnp.bfloat16)


def own_rows(source, unit_ref, half_rows, span):
    first = pl.multiple_of(lax.axis_index("tm") * half_rows, half_rows)
    return unit_ref[source, pl.ds(first, half_rows), span]


def fine_steps(sign):
    return range(1, FINE + 1) if sign > 0 else range(-FINE, 0)


def prepare(source, sign, unit_ref, left_ref, half_rows):
    length = unit_ref.shape[2] // 2
    for window in range(2):
        span = slice(window * length, (window + 1) * length)
        rows = own_rows(source, unit_ref, half_rows, span)
        for row, step in enumerate(fine_steps(sign)):
            left_ref[row * half_rows : (row + 1) * half_rows, span] = shifted(rows, step)


def coarse_rows(tall_ref, partner, window, amount):
    length = tall_ref.shape[3] - 2 * MARGIN
    phase = amount // FINE % 2
    first = MARGIN + amount - FINE * phase
    return tall_ref[partner, window, phase, first : first + length]


def coarse_columns(tall_ref, partner, amounts):
    return jnp.concatenate(
        [
            jnp.concatenate(
                [coarse_rows(tall_ref, partner, window, amount) for amount in amounts], axis=1
            )
            for window in range(2)
        ],
        axis=0,
    )


def correlate(sign, factor, partner, left_ref, tall_ref, stage_ref):
    half_rows, channels = stage_ref.shape[1:]
    amounts = [sign * FINE * place for place in range(COARSE)]
    steps = fine_steps(sign)
    for column in range(0, COARSE, WIDE):
        right = coarse_columns(tall_ref, partner, amounts[column : column + WIDE])
        for row in range(0, FINE, TALL):
            result = jnp.dot(
                left_ref[row * half_rows : (row + TALL) * half_rows, :], right,
                preferred_element_type=jnp.float32,
            )
            for i, amount in enumerate(amounts[column : column + WIDE]):
                for j, step in enumerate(steps[row : row + TALL]):
                    stage_ref[LAG + amount + step] = factor * result[
                        j * half_rows : (j + 1) * half_rows, i * channels : (i + 1) * channels
                    ]


def early_kernel(pairs_ref, count_ref, taps_ref, *refs):
    blocks, (band_ref, unit_ref, tall_ref) = refs[:3], refs[3:]
    make_band(taps_ref, band_ref)
    for block, (place, window) in zip(blocks, ((OWN, 0), (OWN, 1), (DIAGONAL, 0))):
        normalise(block, band_ref, unit_ref, tall_ref, place, window)


def filter_kernel(units, band_ref, *refs):
    blocks, (unit_ref, tall_ref) = refs[: len(units)], refs[len(units) + 2 :]
    for block, (place, window) in zip(blocks, units):
        normalise(block, band_ref, unit_ref, tall_ref, place, window)


def stack_kernel(scale, units, pairs_ref, count_ref, band_ref, *refs):
    blocks, refs = refs[: len(units)], refs[len(units) + 2 :]
    unit_ref, tall_ref, out_ref, left_ref, stage_ref, sems = refs
    for block, (place, window) in zip(blocks, units):
        normalise(block, band_ref, unit_ref, tall_ref, place, window)
    slots, lags, half_rows, _ = out_ref.shape
    owner = lax.axis_index("chan")

    def ready(slot):
        if slot < slots:
            source = place_of(pairs_ref[0, slot], owner)
            for side, sign in enumerate((1, -1)):
                prepare(source, sign, unit_ref, left_ref.at[slot % 2, side], half_rows)

    copies = []

    def send(slot, first, count):
        span = pl.ds(first, count)
        copy = pltpu.make_async_copy(
            stage_ref.at[slot, span], out_ref.at[slot, span], sems.at[len(copies)]
        )
        copy.start()
        copies.append(copy)

    ready(0)
    for slot in range(slots):
        ready(slot + 1)
        factor = jnp.where(slot < count_ref[0], scale, 0.0)
        source = place_of(pairs_ref[0, slot], owner)
        partner = place_of(pairs_ref[1, slot], owner)
        for side, sign in enumerate((1, -1)):
            correlate(
                sign, factor, partner, left_ref.at[slot % 2, side], tall_ref, stage_ref.at[slot]
            )
            if sign > 0:
                stage_ref[slot, LAG] = factor * jnp.dot(
                    own_rows(source, unit_ref, half_rows, slice(None)),
                    coarse_columns(tall_ref, partner, [0]), preferred_element_type=jnp.float32,
                )
                if slot == slots - 1:
                    send(slot, LAG, lags - LAG)
        if slot == slots - 1:
            send(slot, 0, LAG)
        else:
            send(slot, 0, lags)
    for copy in copies:
        copy.wait()


def body(traces, fir_taps, pair_blocks, pair_count):
    rows, windows, length = traces.shape
    own = traces.reshape(rows, length)
    halves = lax.axis_size("tm")
    cap = pair_blocks.shape[0]
    lags = 2 * LAG + 1
    half_rows = rows // halves
    scale = float(windows * halves * length) ** (-0.5)

    swap = lambda array: passed(array, "tm", lambda i: 1 - i)
    partner = passed(own, "chan", partner_of)
    below = passed(own, "chan", lambda i: i + REACH)
    above = passed(own, "chan", lambda i: i - REACH)
    diagonal = passed(own, "chan", diagonal_of)
    pairs, count = pair_blocks.T, pair_count
    taps = fir_taps.astype(jnp.float32)[None, :]

    smem = pl.BlockSpec(memory_space=pltpu.SMEM)
    vmem = pl.BlockSpec(memory_space=pltpu.VMEM)
    hbm = pl.BlockSpec(memory_space=pl.ANY)
    params = pltpu.CompilerParams(vmem_limit_bytes=32 * 1024 * 1024)
    band_shape = jax.ShapeDtypeStruct((2, TILE, TILE), jnp.bfloat16)
    unit_shape = jax.ShapeDtypeStruct((NEAR, rows, halves * length), jnp.bfloat16)
    tall_shape = jax.ShapeDtypeStruct(
        (NEAR, halves, 2, length + 2 * MARGIN, rows), jnp.bfloat16
    )
    out_shape = jax.ShapeDtypeStruct((cap, lags, half_rows, rows), jnp.float32)
    light = pl.CostEstimate(flops=1, bytes_accessed=1, transcendentals=0)
    heavy = pl.CostEstimate(
        flops=2 * cap * lags * half_rows * rows * halves * length,
        bytes_accessed=cap * lags * half_rows * rows * 4,
        transcendentals=0,
    )

    band, unit, tall = pl.pallas_call(
        early_kernel,
        out_shape=(band_shape, unit_shape, tall_shape),
        in_specs=[smem, smem] + [vmem] * 4,
        out_specs=(vmem, vmem, vmem),
        compiler_params=params,
        cost_estimate=light,
    )(pairs, count, taps, own, swap(own), diagonal)

    def more(units, blocks, unit, tall):
        return pl.pallas_call(
            functools.partial(filter_kernel, units),
            out_shape=(unit_shape, tall_shape),
            in_specs=[vmem] * (len(units) + 3),
            out_specs=(vmem, vmem),
            input_output_aliases={len(units) + 1: 0, len(units) + 2: 1},
            compiler_params=params,
            cost_estimate=light,
        )(band, *blocks, unit, tall)

    mine, other = 0, 1
    sent, band = lax.optimization_barrier((diagonal, band))
    unit, tall = more(
        ((BELOW, mine), (ABOVE, mine), (PARTNER, mine), (DIAGONAL, other)),
        (below, above, partner, swap(sent)), unit, tall,
    )
    units = ((BELOW, other), (ABOVE, other), (PARTNER, other))
    _, _, out = pl.pallas_call(
        functools.partial(stack_kernel, scale, units),
        out_shape=(unit_shape, tall_shape, out_shape),
        in_specs=[smem, smem] + [vmem] * (len(units) + 3),
        out_specs=(vmem, vmem, hbm),
        input_output_aliases={len(units) + 3: 0, len(units) + 4: 1},
        scratch_shapes=[
            pltpu.VMEM((2, 2, FINE * half_rows, halves * length), jnp.bfloat16),
            pltpu.VMEM((cap, lags, half_rows, rows), jnp.float32),
            pltpu.SemaphoreType.DMA((cap + 1,)),
        ],
        compiler_params=params,
        cost_estimate=heavy,
    )(pairs, count, band, swap(below), swap(above), swap(partner), unit, tall)
    return jnp.transpose(out, (0, 2, 1, 3))


def solution(mesh):
    return jax.shard_map(
        body,
        mesh=mesh,
        in_specs=(
            P(("groups", "chan"), "tm", None),
            P(),
            P(("groups", "chan"), None),
            P(("groups", "chan")),
        ),
        out_specs=P(("groups", "chan"), "tm", None, None),
        check_vma=False,
    )
```

```python
import functools

import jax
import jax.numpy as jnp
from jax import lax
from jax.experimental import pallas as pl
from jax.experimental.pallas import tpu as pltpu
from jax.sharding import PartitionSpec as P

LAG = 32
REACH = 2
NEAR = 2 * REACH + 1
FINE = 8
COARSE = LAG // FINE
LANES = 128
TILE = 256
MARGIN = 32
OWN, PARTNER, BELOW, ABOVE, DIAGONAL = range(NEAR)


def passed(block, axis, target):
    size = lax.axis_size(axis)
    route = [(i, target(i)) for i in range(size) if 0 <= target(i) < size]
    return lax.ppermute(block, axis, route)


def partner_of(i):
    return i + 1 if i % 2 == 0 else i - 1


def diagonal_of(i):
    return i - 1 if i % 2 == 0 else i + 1


def place_of(block, owner):
    offset = block - owner
    side = jnp.where(offset == 1 - 2 * lax.rem(owner, 2), PARTNER, DIAGONAL)
    away = jnp.where(offset == -REACH, BELOW, jnp.where(offset == REACH, ABOVE, side))
    return jnp.where(offset == 0, OWN, away)


def shifted(rows, amount):
    if amount == 0:
        return rows
    length = rows.shape[-1]
    moved = pltpu.roll(rows, amount % length, 1)
    edge = slice(0, LANES) if amount > 0 else slice(length - LANES, length)
    lane = lax.broadcasted_iota(jnp.int32, (rows.shape[0], LANES), 1)
    keep = lane >= amount if amount > 0 else lane < LANES + amount
    cut = jnp.where(keep, moved[:, edge], jnp.zeros((), rows.dtype))
    if amount > 0:
        return jnp.concatenate([cut, moved[:, LANES:]], axis=1)
    return jnp.concatenate([moved[:, : length - LANES], cut], axis=1)


def make_band(taps_ref, band_ref):
    taps = taps_ref[...]
    wide = jnp.concatenate([taps, jnp.zeros((1, TILE - taps.shape[1]), jnp.float32)], axis=1)
    band = pltpu.roll(jnp.broadcast_to(wide, (TILE, TILE)), 0, 1, stride=1, stride_axis=0)
    row = lax.broadcasted_iota(jnp.int32, (TILE, TILE), 0)
    column = lax.broadcasted_iota(jnp.int32, (TILE, TILE), 1)
    band_ref[0] = jnp.where(column >= row, band, 0.0).astype(jnp.bfloat16)
    band_ref[1] = jnp.where(column < row, band, 0.0).astype(jnp.bfloat16)


def normalise(source_ref, band_ref, unit_ref, tall_ref, place, window):
    rows, length = unit_ref.shape[1], source_ref.shape[-1]
    tiles = length // TILE
    stacked = jnp.concatenate(
        [source_ref[:rows, tile * TILE : (tile + 1) * TILE] for tile in range(tiles)], axis=0
    )
    here = jnp.dot(stacked, band_ref[0], preferred_element_type=jnp.float32)
    after = jnp.dot(stacked[:-rows], band_ref[1], preferred_element_type=jnp.float32)
    pieces = [here[:rows]] + [
        here[tile * rows : (tile + 1) * rows] + after[(tile - 1) * rows : tile * rows]
        for tile in range(1, tiles)
    ]
    filtered = jnp.concatenate(pieces, axis=1)
    meansq = jnp.mean(filtered * filtered, axis=-1, keepdims=True)
    unit = filtered * lax.rsqrt(meansq + 1e-06)
    unit_ref[place, :, window * length : (window + 1) * length] = unit.astype(jnp.bfloat16)
    tall = unit.T
    gap = jnp.zeros((FINE, rows), jnp.float32)
    edge = jnp.zeros((MARGIN, rows), jnp.bfloat16)
    inner = MARGIN - 2 * FINE
    for phase in range(2):
        tall_ref[place, window, phase, :MARGIN] = edge
        tall_ref[place, window, phase, length + MARGIN :] = edge
    tall_ref[place, window, 0, MARGIN : MARGIN + length] = tall.astype(jnp.bfloat16)
    tall_ref[place, window, 1, inner : inner + length + 2 * FINE] = jnp.concatenate(
        [gap, tall, gap], axis=0
    ).astype(jnp.bfloat16)


def own_rows(source, unit_ref, half_rows, span):
    first = pl.multiple_of(lax.axis_index("tm") * half_rows, half_rows)
    return unit_ref[source, pl.ds(first, half_rows), span]


def fine_steps(sign):
    return range(1, FINE + 1) if sign > 0 else range(-FINE, 0)


def prepare(source, sign, unit_ref, left_ref, half_rows):
    length = unit_ref.shape[2] // 2
    for window in range(2):
        span = slice(window * length, (window + 1) * length)
        rows = own_rows(source, unit_ref, half_rows, span)
        for row, step in enumerate(fine_steps(sign)):
            left_ref[row * half_rows : (row + 1) * half_rows, span] = shifted(rows, step)


def coarse_rows(tall_ref, partner, window, amount):
    length = tall_ref.shape[3] - 2 * MARGIN
    phase = amount // FINE % 2
    first = MARGIN + amount - FINE * phase
    return tall_ref[partner, window, phase, first : first + length]


def coarse_columns(tall_ref, partner, amounts):
    return jnp.concatenate(
        [
            jnp.concatenate(
                [coarse_rows(tall_ref, partner, window, amount) for amount in amounts], axis=1
            )
            for window in range(2)
        ],
        axis=0,
    )


def correlate(sign, factor, partner, left_ref, tall_ref, stage_ref):
    half_rows, channels = stage_ref.shape[1:]
    amounts = [sign * FINE * place for place in range(COARSE)]
    result = jnp.dot(
        left_ref[...], coarse_columns(tall_ref, partner, amounts),
        preferred_element_type=jnp.float32,
    )
    for column, amount in enumerate(amounts):
        for row, step in enumerate(fine_steps(sign)):
            stage_ref[LAG + amount + step] = factor * result[
                row * half_rows : (row + 1) * half_rows,
                column * channels : (column + 1) * channels,
            ]


def early_kernel(pairs_ref, count_ref, taps_ref, *refs):
    blocks, (band_ref, unit_ref, tall_ref) = refs[:3], refs[3:]
    make_band(taps_ref, band_ref)
    for block, (place, window) in zip(blocks, ((OWN, 0), (OWN, 1), (DIAGONAL, 0))):
        normalise(block, band_ref, unit_ref, tall_ref, place, window)


def filter_kernel(units, band_ref, *refs):
    blocks, (unit_ref, tall_ref) = refs[: len(units)], refs[len(units) + 2 :]
    for block, (place, window) in zip(blocks, units):
        normalise(block, band_ref, unit_ref, tall_ref, place, window)


def stack_kernel(scale, units, pairs_ref, count_ref, band_ref, *refs):
    blocks, refs = refs[: len(units)], refs[len(units) + 2 :]
    unit_ref, tall_ref, out_ref, left_ref, stage_ref, sems = refs
    for block, (place, window) in zip(blocks, units):
        normalise(block, band_ref, unit_ref, tall_ref, place, window)
    slots, lags, half_rows, _ = out_ref.shape
    owner = lax.axis_index("chan")

    def ready(slot, side, sign):
        if slot < slots:
            source = place_of(pairs_ref[0, slot], owner)
            prepare(source, sign, unit_ref, left_ref.at[slot % 2, side], half_rows)

    def piece(slot, side):
        span = pl.ds(LAG, lags - LAG) if side == 0 else pl.ds(0, LAG)
        return pltpu.make_async_copy(
            stage_ref.at[slot, span], out_ref.at[slot, span], sems.at[slot, side]
        )

    for side, sign in enumerate((1, -1)):
        ready(0, side, sign)
    for slot in range(slots):

        @pl.when(slot < count_ref[0])
        def _():
            source = place_of(pairs_ref[0, slot], owner)
            partner = place_of(pairs_ref[1, slot], owner)
            for side, sign in enumerate((1, -1)):
                ready(slot + 1, side, sign)
                correlate(
                    sign, scale, partner, left_ref.at[slot % 2, side], tall_ref,
                    stage_ref.at[slot],
                )
                if sign > 0:
                    stage_ref[slot, LAG] = scale * jnp.dot(
                        own_rows(source, unit_ref, half_rows, slice(None)),
                        coarse_columns(tall_ref, partner, [0]),
                        preferred_element_type=jnp.float32,
                    )
                piece(slot, side).start()

        @pl.when(slot >= count_ref[0])
        def _():
            stage_ref[slot] = jnp.zeros(stage_ref.shape[1:], jnp.float32)
            for side in range(2):
                piece(slot, side).start()

    for slot in range(slots):
        for side in range(2):
            piece(slot, side).wait()


def body(traces, fir_taps, pair_blocks, pair_count):
    rows, windows, length = traces.shape
    own = traces.reshape(rows, length)
    halves = lax.axis_size("tm")
    cap = pair_blocks.shape[0]
    lags = 2 * LAG + 1
    half_rows = rows // halves
    scale = float(windows * halves * length) ** (-0.5)

    swap = lambda array: passed(array, "tm", lambda i: 1 - i)
    partner = passed(own, "chan", partner_of)
    below = passed(own, "chan", lambda i: i + REACH)
    above = passed(own, "chan", lambda i: i - REACH)
    diagonal = passed(own, "chan", diagonal_of)
    pairs, count = pair_blocks.T, pair_count
    taps = fir_taps.astype(jnp.float32)[None, :]

    smem = pl.BlockSpec(memory_space=pltpu.SMEM)
    vmem = pl.BlockSpec(memory_space=pltpu.VMEM)
    hbm = pl.BlockSpec(memory_space=pl.ANY)
    params = pltpu.CompilerParams(vmem_limit_bytes=32 * 1024 * 1024)
    band_shape = jax.ShapeDtypeStruct((2, TILE, TILE), jnp.bfloat16)
    unit_shape = jax.ShapeDtypeStruct((NEAR, rows, halves * length), jnp.bfloat16)
    tall_shape = jax.ShapeDtypeStruct(
        (NEAR, halves, 2, length + 2 * MARGIN, rows), jnp.bfloat16
    )
    out_shape = jax.ShapeDtypeStruct((cap, lags, half_rows, rows), jnp.float32)
    light = pl.CostEstimate(flops=1, bytes_accessed=1, transcendentals=0)
    heavy = pl.CostEstimate(
        flops=2 * cap * lags * half_rows * rows * halves * length,
        bytes_accessed=cap * lags * half_rows * rows * 4,
        transcendentals=0,
    )

    band, unit, tall = pl.pallas_call(
        early_kernel,
        out_shape=(band_shape, unit_shape, tall_shape),
        in_specs=[smem, smem] + [vmem] * 4,
        out_specs=(vmem, vmem, vmem),
        compiler_params=params,
        cost_estimate=light,
    )(pairs, count, taps, own, swap(own), diagonal)

    def more(units, blocks, unit, tall):
        return pl.pallas_call(
            functools.partial(filter_kernel, units),
            out_shape=(unit_shape, tall_shape),
            in_specs=[vmem] * (len(units) + 3),
            out_specs=(vmem, vmem),
            input_output_aliases={len(units) + 1: 0, len(units) + 2: 1},
            compiler_params=params,
            cost_estimate=light,
        )(band, *blocks, unit, tall)

    mine, other = 0, 1
    sent, band = lax.optimization_barrier((diagonal, band))
    unit, tall = more(
        ((BELOW, mine), (ABOVE, mine), (PARTNER, mine), (DIAGONAL, other)),
        (below, above, partner, swap(sent)), unit, tall,
    )
    units = ((BELOW, other), (ABOVE, other), (PARTNER, other))
    _, _, out = pl.pallas_call(
        functools.partial(stack_kernel, scale, units),
        out_shape=(unit_shape, tall_shape, out_shape),
        in_specs=[smem, smem] + [vmem] * (len(units) + 3),
        out_specs=(vmem, vmem, hbm),
        input_output_aliases={len(units) + 3: 0, len(units) + 4: 1},
        scratch_shapes=[
            pltpu.VMEM((2, 2, FINE * half_rows, halves * length), jnp.bfloat16),
            pltpu.VMEM((cap, lags, half_rows, rows), jnp.float32),
            pltpu.SemaphoreType.DMA((cap, 2)),
        ],
        compiler_params=params,
        cost_estimate=heavy,
    )(pairs, count, band, swap(below), swap(above), swap(partner), unit, tall)
    return jnp.transpose(out, (0, 2, 1, 3))


def solution(mesh):
    return jax.shard_map(
        body,
        mesh=mesh,
        in_specs=(
            P(("groups", "chan"), "tm", None),
            P(),
            P(("groups", "chan"), None),
            P(("groups", "chan")),
        ),
        out_specs=P(("groups", "chan"), "tm", None, None),
        check_vma=False,
    )
```

```python
import functools

import jax
import jax.numpy as jnp
from jax import lax
from jax.experimental import pallas as pl
from jax.experimental.pallas import tpu as pltpu
from jax.sharding import PartitionSpec as P

LAG = 32
REACH = 2
NEAR = 2 * REACH + 1
FINE = 8
COARSE = LAG // FINE
LANES = 128
TILE = 256
MARGIN = 32
OWN, PARTNER, BELOW, ABOVE, DIAGONAL = range(NEAR)


def passed(block, axis, target):
    size = lax.axis_size(axis)
    route = [(i, target(i)) for i in range(size) if 0 <= target(i) < size]
    return lax.ppermute(block, axis, route)


def partner_of(i):
    return i + 1 if i % 2 == 0 else i - 1


def diagonal_of(i):
    return i - 1 if i % 2 == 0 else i + 1


def place_of(block, owner):
    offset = block - owner
    side = jnp.where(offset == 1 - 2 * lax.rem(owner, 2), PARTNER, DIAGONAL)
    away = jnp.where(offset == -REACH, BELOW, jnp.where(offset == REACH, ABOVE, side))
    return jnp.where(offset == 0, OWN, away)


def shifted(rows, amount):
    if amount == 0:
        return rows
    length = rows.shape[-1]
    moved = pltpu.roll(rows, amount % length, 1)
    edge = slice(0, LANES) if amount > 0 else slice(length - LANES, length)
    lane = lax.broadcasted_iota(jnp.int32, (rows.shape[0], LANES), 1)
    keep = lane >= amount if amount > 0 else lane < LANES + amount
    cut = jnp.where(keep, moved[:, edge], jnp.zeros((), rows.dtype))
    if amount > 0:
        return jnp.concatenate([cut, moved[:, LANES:]], axis=1)
    return jnp.concatenate([moved[:, : length - LANES], cut], axis=1)


def make_band(taps_ref, band_ref):
    taps = taps_ref[...]
    wide = jnp.concatenate([taps, jnp.zeros((1, TILE - taps.shape[1]), jnp.float32)], axis=1)
    band = pltpu.roll(jnp.broadcast_to(wide, (TILE, TILE)), 0, 1, stride=1, stride_axis=0)
    row = lax.broadcasted_iota(jnp.int32, (TILE, TILE), 0)
    column = lax.broadcasted_iota(jnp.int32, (TILE, TILE), 1)
    band_ref[0] = jnp.where(column >= row, band, 0.0).astype(jnp.bfloat16)
    band_ref[1] = jnp.where(column < row, band, 0.0).astype(jnp.bfloat16)


def normalise(source_ref, band_ref, unit_ref, tall_ref, place, window):
    rows, length = unit_ref.shape[1], source_ref.shape[-1]
    tiles = length // TILE
    stacked = jnp.concatenate(
        [source_ref[:rows, tile * TILE : (tile + 1) * TILE] for tile in range(tiles)], axis=0
    )
    here = jnp.dot(stacked, band_ref[0], preferred_element_type=jnp.float32)
    after = jnp.dot(stacked[:-rows], band_ref[1], preferred_element_type=jnp.float32)
    pieces = [here[:rows]] + [
        here[tile * rows : (tile + 1) * rows] + after[(tile - 1) * rows : tile * rows]
        for tile in range(1, tiles)
    ]
    filtered = jnp.concatenate(pieces, axis=1)
    meansq = jnp.mean(filtered * filtered, axis=-1, keepdims=True)
    unit = filtered * lax.rsqrt(meansq + 1e-06)
    unit_ref[place, :, window * length : (window + 1) * length] = unit.astype(jnp.bfloat16)
    tall = unit.T
    gap = jnp.zeros((FINE, rows), jnp.float32)
    edge = jnp.zeros((MARGIN, rows), jnp.bfloat16)
    inner = MARGIN - 2 * FINE
    for phase in range(2):
        tall_ref[place, window, phase, :MARGIN] = edge
        tall_ref[place, window, phase, length + MARGIN :] = edge
    tall_ref[place, window, 0, MARGIN : MARGIN + length] = tall.astype(jnp.bfloat16)
    tall_ref[place, window, 1, inner : inner + length + 2 * FINE] = jnp.concatenate(
        [gap, tall, gap], axis=0
    ).astype(jnp.bfloat16)


def own_rows(source, unit_ref, half_rows, span):
    first = pl.multiple_of(lax.axis_index("tm") * half_rows, half_rows)
    return unit_ref[source, pl.ds(first, half_rows), span]


def fine_steps(sign):
    return range(1, FINE + 1) if sign > 0 else range(-FINE, 0)


def prepare(source, sign, unit_ref, left_ref, half_rows):
    length = unit_ref.shape[2] // 2
    for window in range(2):
        span = slice(window * length, (window + 1) * length)
        rows = own_rows(source, unit_ref, half_rows, span)
        for row, step in enumerate(fine_steps(sign)):
            left_ref[row * half_rows : (row + 1) * half_rows, span] = shifted(rows, step)


def coarse_rows(tall_ref, partner, window, amount):
    length = tall_ref.shape[3] - 2 * MARGIN
    phase = amount // FINE % 2
    first = MARGIN + amount - FINE * phase
    return tall_ref[partner, window, phase, first : first + length]


def coarse_columns(tall_ref, partner, amounts):
    return jnp.concatenate(
        [
            jnp.concatenate(
                [coarse_rows(tall_ref, partner, window, amount) for amount in amounts], axis=1
            )
            for window in range(2)
        ],
        axis=0,
    )


def correlate(sign, places, factor, partner, left_ref, tall_ref, stage_ref):
    half_rows, channels = stage_ref.shape[1:]
    amounts = [sign * FINE * place for place in places]
    result = jnp.dot(
        left_ref[...], coarse_columns(tall_ref, partner, amounts),
        preferred_element_type=jnp.float32,
    )
    for column, amount in enumerate(amounts):
        for row, step in enumerate(fine_steps(sign)):
            stage_ref[LAG + amount + step] = factor * result[
                row * half_rows : (row + 1) * half_rows,
                column * channels : (column + 1) * channels,
            ]


def early_kernel(pairs_ref, count_ref, taps_ref, *refs):
    blocks, (band_ref, unit_ref, tall_ref) = refs[:3], refs[3:]
    make_band(taps_ref, band_ref)
    for block, (place, window) in zip(blocks, ((OWN, 0), (OWN, 1), (DIAGONAL, 0))):
        normalise(block, band_ref, unit_ref, tall_ref, place, window)


def filter_kernel(units, band_ref, *refs):
    blocks, (unit_ref, tall_ref) = refs[: len(units)], refs[len(units) + 2 :]
    for block, (place, window) in zip(blocks, units):
        normalise(block, band_ref, unit_ref, tall_ref, place, window)


def stack_kernel(scale, units, pairs_ref, count_ref, band_ref, *refs):
    blocks, refs = refs[: len(units)], refs[len(units) + 2 :]
    unit_ref, tall_ref, out_ref, left_ref, stage_ref, sems = refs
    for block, (place, window) in zip(blocks, units):
        normalise(block, band_ref, unit_ref, tall_ref, place, window)
    slots, lags, half_rows, _ = out_ref.shape
    owner = lax.axis_index("chan")

    def ready(slot):
        if slot < slots:
            source = place_of(pairs_ref[0, slot], owner)
            for side, sign in enumerate((1, -1)):
                prepare(source, sign, unit_ref, left_ref.at[slot % 2, side], half_rows)

    copies = []

    def send(slot, first, count):
        span = pl.ds(first, count)
        copy = pltpu.make_async_copy(
            stage_ref.at[slot, span], out_ref.at[slot, span], sems.at[len(copies)]
        )
        copy.start()
        copies.append(copy)

    ready(0)
    for slot in range(slots):
        ready(slot + 1)
        factor = jnp.where(slot < count_ref[0], scale, 0.0)
        source = place_of(pairs_ref[0, slot], owner)
        partner = place_of(pairs_ref[1, slot], owner)
        last = slot == slots - 1
        whole = range(COARSE)
        correlate(
            1, whole, factor, partner, left_ref.at[slot % 2, 0], tall_ref, stage_ref.at[slot]
        )
        stage_ref[slot, LAG] = factor * jnp.dot(
            own_rows(source, unit_ref, half_rows, slice(None)),
            coarse_columns(tall_ref, partner, [0]), preferred_element_type=jnp.float32,
        )
        if last:
            send(slot, LAG, lags - LAG)
        for places in (whole[: COARSE // 2], whole[COARSE // 2 :]) if last else (whole,):
            correlate(
                -1, places, factor, partner, left_ref.at[slot % 2, 1], tall_ref,
                stage_ref.at[slot],
            )
            if last:
                send(slot, LAG - FINE * (places[-1] + 1), FINE * len(places))
        if not last:
            send(slot, 0, lags)
    for copy in copies:
        copy.wait()


def body(traces, fir_taps, pair_blocks, pair_count):
    rows, windows, length = traces.shape
    own = traces.reshape(rows, length)
    halves = lax.axis_size("tm")
    cap = pair_blocks.shape[0]
    lags = 2 * LAG + 1
    half_rows = rows // halves
    scale = float(windows * halves * length) ** (-0.5)

    swap = lambda array: passed(array, "tm", lambda i: 1 - i)
    partner = passed(own, "chan", partner_of)
    below = passed(own, "chan", lambda i: i + REACH)
    above = passed(own, "chan", lambda i: i - REACH)
    diagonal = passed(own, "chan", diagonal_of)
    pairs, count = pair_blocks.T, pair_count
    taps = fir_taps.astype(jnp.float32)[None, :]

    smem = pl.BlockSpec(memory_space=pltpu.SMEM)
    vmem = pl.BlockSpec(memory_space=pltpu.VMEM)
    hbm = pl.BlockSpec(memory_space=pl.ANY)
    params = pltpu.CompilerParams(vmem_limit_bytes=32 * 1024 * 1024)
    band_shape = jax.ShapeDtypeStruct((2, TILE, TILE), jnp.bfloat16)
    unit_shape = jax.ShapeDtypeStruct((NEAR, rows, halves * length), jnp.bfloat16)
    tall_shape = jax.ShapeDtypeStruct(
        (NEAR, halves, 2, length + 2 * MARGIN, rows), jnp.bfloat16
    )
    out_shape = jax.ShapeDtypeStruct((cap, lags, half_rows, rows), jnp.float32)
    light = pl.CostEstimate(flops=1, bytes_accessed=1, transcendentals=0)
    heavy = pl.CostEstimate(
        flops=2 * cap * lags * half_rows * rows * halves * length,
        bytes_accessed=cap * lags * half_rows * rows * 4,
        transcendentals=0,
    )

    band, unit, tall = pl.pallas_call(
        early_kernel,
        out_shape=(band_shape, unit_shape, tall_shape),
        in_specs=[smem, smem] + [vmem] * 4,
        out_specs=(vmem, vmem, vmem),
        compiler_params=params,
        cost_estimate=light,
    )(pairs, count, taps, own, swap(own), diagonal)

    def more(units, blocks, unit, tall):
        return pl.pallas_call(
            functools.partial(filter_kernel, units),
            out_shape=(unit_shape, tall_shape),
            in_specs=[vmem] * (len(units) + 3),
            out_specs=(vmem, vmem),
            input_output_aliases={len(units) + 1: 0, len(units) + 2: 1},
            compiler_params=params,
            cost_estimate=light,
        )(band, *blocks, unit, tall)

    mine, other = 0, 1
    sent, band = lax.optimization_barrier((diagonal, band))
    unit, tall = more(
        ((BELOW, mine), (ABOVE, mine), (PARTNER, mine), (DIAGONAL, other)),
        (below, above, partner, swap(sent)), unit, tall,
    )
    units = ((BELOW, other), (ABOVE, other), (PARTNER, other))
    _, _, out = pl.pallas_call(
        functools.partial(stack_kernel, scale, units),
        out_shape=(unit_shape, tall_shape, out_shape),
        in_specs=[smem, smem] + [vmem] * (len(units) + 3),
        out_specs=(vmem, vmem, hbm),
        input_output_aliases={len(units) + 3: 0, len(units) + 4: 1},
        scratch_shapes=[
            pltpu.VMEM((2, 2, FINE * half_rows, halves * length), jnp.bfloat16),
            pltpu.VMEM((cap, lags, half_rows, rows), jnp.float32),
            pltpu.SemaphoreType.DMA((cap + 2,)),
        ],
        compiler_params=params,
        cost_estimate=heavy,
    )(pairs, count, band, swap(below), swap(above), swap(partner), unit, tall)
    return jnp.transpose(out, (0, 2, 1, 3))


def solution(mesh):
    return jax.shard_map(
        body,
        mesh=mesh,
        in_specs=(
            P(("groups", "chan"), "tm", None),
            P(),
            P(("groups", "chan"), None),
            P(("groups", "chan")),
        ),
        out_specs=P(("groups", "chan"), "tm", None, None),
        check_vma=False,
    )
```
